128 devices in a mesh: east: 8 (over x, core), north: 16 (over z, y).
Axes of the slice: x: 4, y: 4, z: 4, core: 2. Of those that a mesh axis runs over, the one named last changes fastest.
Arguments:
- heights: bfloat16 [524288, 128], P(('east', 'north')), may hold values from -6 to 6
- segment_ids: int32 [524288], P(('east', 'north')), may hold values from 0 to 1023
- tile_owner: int32 [524288, 1], P(('east', 'north')), may hold values from 0 to 127; in each aligned block of 4096 rows (0 to 4095, 4096 to 8191, ...) at most 64 rows name the same one
- gap_mask: int32 [2048, 8192], P('east', 'north'), may hold values from 0 to 1
- extinction: float32 [8], replicated, may hold values from 0.5 to 300
- sun_side: int32 [8], replicated, may hold values from 0 to 1
Outputs:
- filled_surface: float32 [2048, 8192], P('east', 'north')
- transmittance: float32 [8, 2048, 8192], P(None, 'east', 'north')
The draws below stay inside these ranges and needn't reach their ends.
Inputs may be any that keep to these rules, and one draw needn't show every extreme that they name: `tile_owner`: the rows of one device name one tile at most 64 times, a bound that some block reaches.
All inputs are finite; a program needn't handle non-finite values.
Results may differ from the reference program's by a relative error of at most 0.0003.
Values may be sent and summed in bfloat16 or wider, within the bound.
No kernel may reach another device: no remote copies, remote signals or barrier semaphores. Data moves between devices by JAX's collectives and lax.ppermute only.
A program may use at most 64 MiB of HBM per device.

```python
import math
import jax
import jax.numpy as jnp
import numpy as np

TX = 256
TY = 512
R_DEV = 4096
NS = 8
STEPS = 20
CAP = 64
SEGS = 1024
NX = 2048
NY = 8192
ROWS = 524288
N_EAST = 8
N_NORTH = 16
DEVICES = 128


def draw_gap_mask(key, part):
    key = jax.random.fold_in(key, 11)
    key_block, key_cell = jax.random.split(key)
    coarse = jax.random.randint(key_block, ((NX + 15) // 16, (NY + 15) // 16), 0, 100)
    blocks = jnp.repeat(jnp.repeat(coarse < 35, 16, axis=0), 16, axis=1)[:NX, :NY]
    speckle = jax.random.randint(key_cell, (NX, NY), 0, 100) < 10
    return (blocks | speckle).astype(jnp.int32)


def set_ends(values, rng, low, high):
    longest = values.shape.index(max(values.shape))
    spots = []
    for shift in (0, 1):
        where = [jax.random.randint(jax.random.fold_in(rng, axis), (), 0, length) for axis, length in enumerate(values.shape)]
        where[longest] = (where[longest] + shift) % values.shape[longest]
        spots.append(tuple(where))
    return values.at[spots[0]].set(low).at[spots[1]].set(high)


def level_of(own_key, dims, shards, smallest, top_value):
    level = 1.0
    for dim, shards_of in shards:
        steps = jax.random.uniform(jax.random.fold_in(jax.random.fold_in(own_key, 6), dim), (shards_of,), jnp.float32, smallest / len(shards), top_value / len(shards))
        level = level * jnp.repeat(jnp.exp(steps), dims[dim] // shards_of).reshape((-1,) + (1,) * (len(dims) - 1 - dim))
    return level


def deal_out(rng, own, number, rows, count, top, most, lean):
    order = jax.random.permutation(rng, count)
    packed, ordinary = shares(count, rows * top, most, lean, True), shares(count, rows * top, most, lean, False)
    places = jnp.arange(count)

    def named(lengths, rotation):
        used = int((lengths > 0).sum())
        fixed = max(1, used // 4)
        shifted = fixed + (places - fixed + rotation * (used - fixed)) % max(1, count - fixed)
        return jnp.zeros((count,), jnp.int32).at[order[jnp.where(places < fixed, places, shifted)]].set(jnp.asarray(lengths, jnp.int32))

    lengths = jnp.where(number % 4 == 0, named(packed, number // 4), named(ordinary, number - number // 4 - 1))
    mixed = jax.random.permutation(jax.random.fold_in(own, 3), count)
    donor, receiver = mixed[0:count // 2 * 2:2], mixed[1:count // 2 * 2:2]
    room = jnp.minimum(lengths[donor] - 1, most - lengths[receiver]) // 2
    room = jnp.where((donor == order[0]) | (receiver == order[0]) | (lengths[receiver] == 0), 0, jnp.maximum(room, 0))
    shifted = jax.random.randint(jax.random.fold_in(own, 4), (count // 2,), 0, 1 << 20) % (room + 1)
    lengths = lengths.at[donor].add(-shifted).at[receiver].add(shifted)
    items = jnp.searchsorted(jnp.cumsum(lengths), jnp.arange(rows * top), side="right").astype(jnp.int32)
    listing = items.reshape(top, rows).T
    listing = listing[jax.random.permutation(jax.random.fold_in(own, 1), rows)]
    rotation = jax.random.randint(jax.random.fold_in(own, 2), (rows, 1), 0, top)
    return jnp.take_along_axis(listing, (jnp.arange(top)[None, :] + rotation) % top, axis=1)


def shares(amount, total, reach, skew, full):
    weights = [(1 << 20) // math.isqrt(grade ** skew) + 1 for grade in range(1, amount + 1)]
    largest = reach if full else min(reach, max(-(-total // amount), total * weights[0] // sum(weights)))
    least = 1 if total - largest >= amount - 1 else 0
    counts, rest = [largest] + [least] * (amount - 1), total - largest - least * (amount - 1)
    while rest > 0:
        candidates = [i for i in range(1, amount) if counts[i] < largest] or [i for i in range(1, amount) if counts[i] < reach]
        mass, remaining = sum([weights[i] for i in candidates]), rest
        for i in candidates:
            more = min(reach - counts[i], max(1, remaining * weights[i] // mass), rest)
            counts[i] = counts[i] + more
            rest = rest - more
    return np.array(counts)


def gaussian(stream_key, shape, width, limit, shards=(), held_as=jnp.bfloat16):
    drawn = jax.random.normal(stream_key, shape, jnp.float32) * width
    if len(shards) > 0:
        drawn = level_of(stream_key, shape, shards, -0.22, 0.18) * drawn
    return jnp.clip(drawn, min=-limit, max=limit).astype(held_as)


def setup_inputs(seed: int = 0) -> dict:
    seeds = jax.random.split(jax.random.key(seed), 7)
    heights = gaussian(seeds[0], (ROWS, 128), 1.0, 6.0, ((0, 128),))
    segment_ids = set_ends(jax.random.randint(seeds[1], (ROWS,), 0, SEGS), jax.random.fold_in(seeds[1], 1), 0, SEGS - 1).astype(jnp.int32)
    tile_owner_keys = jax.random.split(jax.random.fold_in(seeds[2], 1), ROWS // R_DEV)
    tile_owner_turns = jax.random.permutation(jax.random.fold_in(seeds[2], 3), ROWS // R_DEV)
    tile_owner = jax.vmap(lambda own, number: deal_out(jax.random.fold_in(seeds[2], 2), own, number, R_DEV, DEVICES, 1, CAP, 2))(tile_owner_keys, tile_owner_turns).reshape((ROWS, 1))
    gap_mask = draw_gap_mask(jax.random.fold_in(seeds[6], 71), 0)
    extinction = jnp.clip(jnp.exp(jax.random.uniform(seeds[4], (NS,), jnp.float32, math.log(0.5), math.log(300.0))), 0.5, 300.0)
    sun_side = set_ends(jax.random.randint(seeds[5], (NS,), 0, 2), jax.random.fold_in(seeds[5], 1), 0, 1).astype(jnp.int32)
    return dict(heights=heights, segment_ids=segment_ids, tile_owner=tile_owner, gap_mask=gap_mask, extinction=extinction, sun_side=sun_side)


def spread_tiles(field):
    return field.reshape(N_EAST, N_NORTH, TX, TY).transpose(0, 2, 1, 3).reshape(NX, NY)


def reference(heights, segment_ids, tile_owner, gap_mask, extinction, sun_side):
    tile_count = N_EAST * N_NORTH
    where_to = tile_owner[:, 0] * SEGS + segment_ids
    summed = jax.ops.segment_sum(heights.astype(jnp.float32), where_to, num_segments=tile_count * SEGS)
    counted = jax.ops.segment_sum(jnp.ones(where_to.shape, jnp.float32), where_to, num_segments=tile_count * SEGS)
    summed = spread_tiles(summed)
    counted = spread_tiles(jnp.broadcast_to(counted[:, None], (tile_count * SEGS, 128)))
    unknown = jnp.where((gap_mask == 1) | (counted == 0.0), 1.0, 0.0).astype(jnp.float32)
    surface = jnp.where(unknown > 0.0, 0.0, summed / jnp.maximum(counted, 1.0)).astype(jnp.float32)
    for repeat_index in range(STEPS):
        padded = jnp.pad(surface, 1)
        beside_all = 0.25 * (padded[2:, 1:-1] + padded[:-2, 1:-1] + padded[1:-1, 2:] + padded[1:-1, :-2])
        surface = surface + unknown * 0.9 * (beside_all - surface)
    optical = (extinction / NY)[:, None, None] * jax.nn.softplus(surface)[None]
    forward = jnp.cumsum(optical, axis=2) - optical
    backward = jnp.flip(jnp.cumsum(jnp.flip(optical, 2), axis=2), 2) - optical
    exposure = jnp.where(sun_side[:, None, None] == 1, backward, forward)
    return surface, jnp.exp(-exposure)
```

```python
import jax
import jax.numpy as jnp
from jax import lax
from jax.experimental import pallas as pl
from jax.experimental.pallas import tpu as pltpu
from jax.sharding import PartitionSpec as P

NS = 8
STEPS = 20
CAP = 64
BLOCK = 72
HALO = 24
GAP = 1000.0

F32 = jnp.float32
BF16 = jnp.bfloat16
I32 = jnp.int32


def vmem():
    return pl.BlockSpec(memory_space=pltpu.VMEM)


def smem():
    return pl.BlockSpec(memory_space=pltpu.SMEM)


def iota(shape, dim):
    return lax.broadcasted_iota(I32, shape, dim)


def deal_kernel(heights, owner, segment, out, wide, dealt, slots, ids, slots_s, sem):
    devices = out.shape[0]
    rows = heights.shape[0]
    chunks = rows // 128
    zeros = jnp.zeros((BLOCK, 128), F32)

    @pl.loop(0, devices)
    def _(t):
        dealt[pl.ds(pl.multiple_of(t * BLOCK, 8), BLOCK), :] = zeros

    @pl.loop(0, rows // 64)
    def _(c):
        at = pl.ds(pl.multiple_of(c * 64, 64), 64)
        wide[at, :] = heights[at, :].astype(F32)

    tile = iota((devices, 128), 0)
    before = (iota((128, 256), 0) < iota((128, 256), 1)).astype(F32).astype(BF16)
    place = iota((128, 128), 0) & (CAP - 1)

    def chunk(c, carry):
        seen, named = carry
        own = owner[pl.ds(c, 1), :]
        hit = tile == own
        counts = jnp.dot(hit.astype(F32).astype(BF16), before, preferred_element_type=F32)
        rank = jnp.sum(jnp.where(hit, counts[:, :128] + seen, 0.0), axis=0, keepdims=True)
        rank = rank.astype(I32)
        slots[pl.ds(c, 1), :] = own * BLOCK + rank
        seg = segment[pl.ds(c, 1), :]
        code = (((seg & 127) + 128) << (seg >> 7)).astype(F32)
        coded = jnp.where(hit, jnp.broadcast_to(code, hit.shape), 0.0).astype(BF16)
        ranked = (place == rank).astype(F32).astype(BF16)
        named = named + lax.dot_general(
            coded, ranked, (((1,), (1,)), ((), ())), preferred_element_type=F32
        )
        return seen + counts[:, 128:], named

    start = jnp.zeros((devices, 128), F32)
    _, named = lax.fori_loop(0, chunks, chunk, (start, start), unroll=2)
    ids[...] = named
    copy = pltpu.make_async_copy(slots, slots_s, sem)
    copy.start()
    copy.wait()

    @pl.loop(0, devices)
    def _(t):
        dealt[pl.ds(t * BLOCK + CAP, 1), :] = ids[pl.ds(t, 1), :]

    @pl.loop(0, chunks)
    def _(c):
        for i in range(128):
            dealt[pl.ds(slots_s[c, i], 1), :] = wide[pl.ds(c * 128 + i, 1), :]

    @pl.loop(0, devices)
    def _(t):
        out[t] = dealt[pl.ds(pl.multiple_of(t * BLOCK, 8), BLOCK), :].astype(BF16)


def bin_kernel(got, gap_mask, out, first, last, acc, codes, lines):
    devices = got.shape[0]
    tile_rows, tile_cols = gap_mask.shape
    quarters = tile_cols // 128
    pairs = devices // 2
    low = iota((1, 128), 1) < CAP
    for p in range(pairs):
        a = got[2 * p][CAP:CAP + 1, :].astype(F32)
        b = got[2 * p + 1][CAP:CAP + 1, :].astype(F32)
        codes[p:p + 1, :] = jnp.where(low, a, b)
    code = codes[...]
    shift = jnp.zeros(code.shape, I32)
    for j in range(1, 8):
        shift = shift + (code >= 128.0 * 2**j).astype(I32)
    seg = (shift << 7) + (code.astype(I32) >> shift) - 128
    for q in range(quarters):
        lines[q] = jnp.where((code > 0.0) & ((seg & (quarters - 1)) == q), seg // quarters, -1)
    acc[...] = jnp.zeros(acc.shape, F32)
    line = iota((tile_rows, 128), 0)
    ones = jnp.ones((256, 128), BF16)

    @pl.loop(0, devices // 4)
    def _(i):
        cells = jnp.concatenate([got[4 * i + j][:CAP, :] for j in range(4)], axis=0)
        cells = jnp.concatenate([cells, ones], axis=1)
        for q in range(quarters):
            hot = jnp.concatenate(
                [
                    (line == lines[q, pl.ds(2 * i + j, 1), :]).astype(F32).astype(BF16)
                    for j in range(2)
                ],
                axis=1,
            )
            acc[q] += jnp.dot(hot, cells, preferred_element_type=F32)

    for q in range(quarters):
        cols = slice(q * 128, (q + 1) * 128)
        total = acc[q]
        summed, counted = total[:, :128], total[:, 128:]
        unknown = (gap_mask[:, cols] == 1) | (counted == 0.0)
        out[:, cols] = jnp.where(unknown, GAP, summed / jnp.maximum(counted, 1.0))
    first[...] = out[:HALO, :]
    last[...] = out[tile_rows - HALO:, :]


def sides_kernel(tile, above, below, west, east, slab):
    rows, cols = tile.shape
    slab[...] = jnp.zeros(slab.shape, F32)
    for out, at, keep in ((west, 0, 0), (east, cols - 128, 128 - HALO)):
        slab[:rows, :] = tile[:, at:at + 128]
        slab[rows:rows + HALO, :] = above[:, at:at + 128]
        slab[rows + HALO:rows + 2 * HALO, :] = below[:, at:at + 128]
        out[...] = slab[...].T[keep:keep + HALO, :]


def fill_kernel(tile, above, below, right, left, surface, depths, totals, cells, rate):
    rows, cols = tile.shape
    wide = cols + 128
    tall = rows + 2 * HALO

    def put(at, width, values):
        unknown = values > 0.5 * GAP
        cells[at, width] = jnp.where(unknown, 0.0, values)
        rate[at, width] = jnp.where(unknown, 0.9, 0.0)

    put(slice(0, rows), slice(0, cols), tile[...])
    put(slice(rows, rows + HALO), slice(0, cols), above[...])
    put(slice(rows + HALO, tall), slice(0, cols), below[...])
    beside = jnp.concatenate(
        [right[...], jnp.zeros((128 - 2 * HALO, right.shape[1]), F32), left[...]], axis=0
    ).T
    put(slice(0, tall), slice(cols, wide), beside[:tall, :])

    blocks = tall // 8
    top = iota((8, wide), 0) == 0
    bottom = iota((8, wide), 0) == 7

    def step(_, carry):
        def block(b):
            return cells[b * 8:b * 8 + 8, :]

        opening = block(0)
        lower_0 = pltpu.roll(opening, 7, axis=0)
        before = pltpu.roll(block(blocks - 1), 1, axis=0)
        here, here_up = opening, lower_0
        for b in range(blocks):
            if b + 1 < blocks:
                after = block(b + 1)
                after_up = pltpu.roll(after, 7, axis=0)
            else:
                after, after_up = opening, lower_0
            here_down = pltpu.roll(here, 1, axis=0)
            total = jnp.where(top, before, here_down) + jnp.where(bottom, after_up, here_up)
            total = total + (pltpu.roll(here, 1, axis=1) + pltpu.roll(here, wide - 1, axis=1))
            cells[b * 8:b * 8 + 8, :] = here + rate[b * 8:b * 8 + 8, :] * (0.25 * total - here)
            before, here, here_up = here_down, after, after_up
        return carry

    lax.fori_loop(0, STEPS, step, 0)
    final = cells[:rows, :cols]
    surface[...] = final
    soft = jnp.maximum(final, 0.0) + jnp.log1p(jnp.exp(-jnp.abs(final)))
    ahead = (iota((cols, cols), 0) < iota((cols, cols), 1)).astype(F32)
    south = jnp.dot(soft, ahead, precision=lax.Precision.HIGHEST, preferred_element_type=F32)
    whole = jnp.sum(soft, axis=1, keepdims=True)
    depths[0] = south
    depths[1] = (whole - south) - soft
    ones = jnp.ones((8, cols), F32)
    along = lax.dot_general(
        ones, soft, (((1,), (1,)), ((), ())), precision=lax.Precision.HIGHEST,
        preferred_element_type=F32,
    )
    packed = jnp.where(iota((8, 128), 0) == 0, along[:, :128], along[:, 128:])
    for n in range(totals.shape[0]):
        totals[n] = packed


def light_kernel(place, extinction, side, depths, totals, out, carried):
    s = pl.program_id(0)
    _, rows, cols = depths.shape
    count = totals.shape[0]

    @pl.when(s == 0)
    def _():
        here = place[0]
        zero = jnp.zeros((8, 128), F32)
        for k in range(2):
            total = zero
            for n in range(count):
                counts = here < n if k else here > n
                total = total + jnp.where(counts, totals[n], zero)
            turned = jnp.concatenate([total, jnp.zeros((120, 128), F32)], axis=0).T
            for half in range(rows // 128):
                carried[k, half * 128:(half + 1) * 128, :] = jnp.broadcast_to(
                    turned[:, half:half + 1], (128, 128)
                )

    pick = side[s]
    rate = -(extinction[s] / (cols * count))
    for q in range(cols // 128):
        at = slice(q * 128, (q + 1) * 128)
        out[0, :, at] = jnp.exp(rate * (depths[pick, :, at] + carried[pick]))


def moved(values, axis, hop):
    count = lax.axis_size(axis)
    return lax.ppermute(
        values, axis, [(i, i + hop) for i in range(count) if 0 <= i + hop < count]
    )


def body(heights, segment_ids, tile_owner, gap_mask, extinction, sun_side):
    rows_here = heights.shape[0]
    tile_rows, tile_cols = gap_mask.shape
    n_north = lax.axis_size("north")
    devices = lax.axis_size("east") * n_north
    chunks = rows_here // 128
    tall = tile_rows + 128
    mib = 1 << 20

    dealt = pl.pallas_call(
        deal_kernel,
        out_shape=jax.ShapeDtypeStruct((devices, BLOCK, 128), BF16),
        in_specs=[vmem()] * 3,
        out_specs=vmem(),
        scratch_shapes=[
            pltpu.VMEM((rows_here, 128), F32),
            pltpu.VMEM((devices * BLOCK, 128), F32),
            pltpu.VMEM((chunks, 128), I32),
            pltpu.VMEM((devices, 128), F32),
            pltpu.SMEM((chunks, 128), I32),
            pltpu.SemaphoreType.DMA,
        ],
        compiler_params=pltpu.CompilerParams(vmem_limit_bytes=24 * mib),
        name="deal",
    )(heights, tile_owner.reshape(chunks, 128), segment_ids.reshape(chunks, 128))

    got = lax.all_to_all(dealt, ("east", "north"), split_axis=0, concat_axis=0, tiled=True)

    strip = jax.ShapeDtypeStruct((HALO, tile_cols), F32)
    tile, first, last = pl.pallas_call(
        bin_kernel,
        out_shape=(jax.ShapeDtypeStruct((tile_rows, tile_cols), F32), strip, strip),
        in_specs=[vmem()] * 2,
        out_specs=(vmem(),) * 3,
        scratch_shapes=[
            pltpu.VMEM((tile_cols // 128, tile_rows, 256), F32),
            pltpu.VMEM((devices // 2, 128), F32),
            pltpu.VMEM((tile_cols // 128, devices // 2, 128), I32),
        ],
        compiler_params=pltpu.CompilerParams(vmem_limit_bytes=24 * mib),
        name="bin",
    )(got, gap_mask)

    below = moved(last, "east", 1)
    above = moved(first, "east", -1)

    turned = jax.ShapeDtypeStruct((HALO, tall), F32)
    west, east = pl.pallas_call(
        sides_kernel,
        out_shape=(turned, turned),
        in_specs=[vmem()] * 3,
        out_specs=(vmem(),) * 2,
        scratch_shapes=[pltpu.VMEM((tall, 128), F32)],
        compiler_params=pltpu.CompilerParams(vmem_limit_bytes=16 * mib),
        name="sides",
    )(tile, above, below)

    left = moved(east, "north", 1)
    right = moved(west, "north", -1)

    surface, depths, totals = pl.pallas_call(
        fill_kernel,
        out_shape=(
            jax.ShapeDtypeStruct((tile_rows, tile_cols), F32),
            jax.ShapeDtypeStruct((2, tile_rows, tile_cols), F32),
            jax.ShapeDtypeStruct((n_north, 8, 128), F32),
        ),
        in_specs=[vmem()] * 5,
        out_specs=(vmem(),) * 3,
        scratch_shapes=[pltpu.VMEM((tile_rows + 2 * HALO, tile_cols + 128), F32)] * 2,
        compiler_params=pltpu.CompilerParams(vmem_limit_bytes=32 * mib),
        name="fill",
    )(tile, above, below, right, left)

    totals = lax.all_to_all(totals, "north", split_axis=0, concat_axis=0, tiled=True)
    place = lax.axis_index("north").astype(I32).reshape(1)

    light = pl.pallas_call(
        light_kernel,
        grid=(NS,),
        out_shape=jax.ShapeDtypeStruct((NS, tile_rows, tile_cols), F32),
        in_specs=[smem()] * 3 + [vmem()] * 2,
        out_specs=pl.BlockSpec((1, tile_rows, tile_cols), lambda s: (s, 0, 0)),
        scratch_shapes=[pltpu.VMEM((2, tile_rows, 128), F32)],
        compiler_params=pltpu.CompilerParams(vmem_limit_bytes=24 * mib),
        name="light",
    )(place, extinction, sun_side, depths, totals)
    return surface, light


def solution(mesh):
    return jax.shard_map(
        body,
        mesh=mesh,
        in_specs=(
            P(("east", "north"), None),
            P(("east", "north")),
            P(("east", "north"), None),
            P("east", "north"),
            P(),
            P(),
        ),
        out_specs=(P("east", "north"), P(None, "east", "north")),
        check_vma=False,
    )
```

```python
import jax
import jax.numpy as jnp
from jax import lax
from jax.experimental import pallas as pl
from jax.experimental.pallas import tpu as pltpu
from jax.sharding import PartitionSpec as P

NS = 8
STEPS = 20
CAP = 64
BLOCK = 72
HALO = 24
GAP = 1000.0
GROUP = 64
UNROLL = 16
PARTS = 4

F32 = jnp.float32
BF16 = jnp.bfloat16
I32 = jnp.int32


def vmem():
    return pl.BlockSpec(memory_space=pltpu.VMEM)


def hbm():
    return pl.BlockSpec(memory_space=pltpu.HBM)


def smem():
    return pl.BlockSpec(memory_space=pltpu.SMEM)


def iota(shape, dim):
    return lax.broadcasted_iota(I32, shape, dim)


def split(values):
    terms = []
    for _ in range(3):
        term = values.astype(BF16)
        terms.append(term)
        values = values - term.astype(F32)
    return terms


def deal_kernel(
    heights_in,
    owner_in,
    segment_in,
    out,
    heights,
    owner,
    segment,
    wide,
    dealt,
    packed,
    slots,
    ids,
    slots_s,
    sems,
):
    devices = out.shape[0]
    rows = heights.shape[0]
    chunks = rows // 128
    half = chunks // 2
    loads = [
        pltpu.make_async_copy(src, dst, sems.at[i])
        for i, (src, dst) in enumerate(
            ((owner_in, owner), (segment_in, segment), (heights_in, heights))
        )
    ]
    for load in loads:
        load.start()
    zeros = jnp.zeros((BLOCK, 128), F32)

    @pl.loop(0, devices, unroll=4)
    def _(t):
        dealt[pl.ds(pl.multiple_of(t * BLOCK, 8), BLOCK), :] = zeros

    tile = iota((devices, 128), 0)
    before = (iota((128, 256), 0) < iota((128, 256), 1)).astype(F32).astype(BF16)
    place = iota((128, 128), 0) & (CAP - 1)
    loads[0].wait()
    loads[1].wait()

    def chunk(c, carry):
        seen, named = carry
        own = owner[pl.ds(c, 1), :]
        hit = tile == own
        counts = jnp.dot(hit.astype(F32).astype(BF16), before, preferred_element_type=F32)
        rank = jnp.sum(jnp.where(hit, counts[:, :128] + seen, 0.0), axis=0, keepdims=True)
        rank = rank.astype(I32)
        slots[pl.ds(c, 1), :] = own * BLOCK + rank
        seg = segment[pl.ds(c, 1), :]
        code = (((seg & 127) + 128) << (seg >> 7)).astype(F32)
        coded = jnp.where(hit, jnp.broadcast_to(code, hit.shape), 0.0).astype(BF16)
        ranked = (place == rank).astype(F32).astype(BF16)
        named = named + lax.dot_general(
            coded, ranked, (((1,), (1,)), ((), ())), preferred_element_type=F32
        )
        return seen + counts[:, 128:], named

    start = jnp.zeros((devices, 128), F32)
    carry = lax.fori_loop(0, half, chunk, (start, start), unroll=UNROLL)
    copies = [
        pltpu.make_async_copy(
            slots.at[pl.ds(i * half, half)], slots_s.at[pl.ds(i * half, half)], sems.at[3 + i]
        )
        for i in range(2)
    ]
    copies[0].start()
    _, named = lax.fori_loop(half, chunks, chunk, carry, unroll=UNROLL)
    ids[...] = named
    copies[1].start()
    loads[2].wait()

    @pl.loop(0, rows // 64, unroll=4)
    def _(c):
        at = pl.ds(pl.multiple_of(c * 64, 64), 64)
        wide[at, :] = heights[at, :].astype(F32)

    @pl.loop(0, devices, unroll=8)
    def _(t):
        dealt[pl.ds(t * BLOCK + CAP, 1), :] = ids[pl.ds(t, 1), :]

    for i in range(2):
        copies[i].wait()

        @pl.loop(i * half, (i + 1) * half)
        def _(c):
            for i in range(128):
                dealt[pl.ds(slots_s[c, i], 1), :] = wide[pl.ds(c * 128 + i, 1), :]

    part = devices // PARTS
    stores = []
    for i in range(PARTS):

        @pl.loop(i * part, (i + 1) * part, unroll=4)
        def _(t):
            packed[t] = dealt[pl.ds(pl.multiple_of(t * BLOCK, 8), BLOCK), :].astype(BF16)

        at = pl.ds(i * part, part)
        stores.append(pltpu.make_async_copy(packed.at[at], out.at[at], sems.at[5 + i]))
        stores[-1].start()
    for store in stores:
        store.wait()


def bin_kernel(got, gap_mask, out, first, last, acc, codes, lines):
    devices = got.shape[0]
    tile_rows, tile_cols = gap_mask.shape
    quarters = tile_cols // 128
    pairs = devices // 2
    low = iota((1, 128), 1) < CAP
    for p in range(pairs):
        a = got[2 * p][CAP:CAP + 1, :].astype(F32)
        b = got[2 * p + 1][CAP:CAP + 1, :].astype(F32)
        codes[p:p + 1, :] = jnp.where(low, a, b)
    code = codes[...]
    shift = jnp.zeros(code.shape, I32)
    for j in range(1, 8):
        shift = shift + (code >= 128.0 * 2**j).astype(I32)
    seg = (shift << 7) + (code.astype(I32) >> shift) - 128
    for q in range(quarters):
        lines[q] = jnp.where((code > 0.0) & ((seg & (quarters - 1)) == q), seg // quarters, -1)
    line = iota((tile_rows, 128), 0)
    ones = jnp.ones((GROUP * CAP, 128), BF16)

    def group(i, fresh):
        cells = jnp.concatenate([got[GROUP * i + j][:CAP, :] for j in range(GROUP)], axis=0)
        cells = jnp.concatenate([cells, ones], axis=1)
        for q in range(quarters):
            hot = jnp.concatenate(
                [
                    (line == lines[q, pl.ds(GROUP // 2 * i + j, 1), :]).astype(F32).astype(BF16)
                    for j in range(GROUP // 2)
                ],
                axis=1,
            )
            part = jnp.dot(hot, cells, preferred_element_type=F32)
            acc[q] = part if fresh else acc[q] + part

    group(0, True)

    @pl.loop(1, devices // GROUP)
    def _(i):
        group(i, False)

    for q in range(quarters):
        cols = slice(q * 128, (q + 1) * 128)
        total = acc[q]
        summed, counted = total[:, :128], total[:, 128:]
        unknown = (gap_mask[:, cols] == 1) | (counted == 0.0)
        out[:, cols] = jnp.where(unknown, GAP, summed / jnp.maximum(counted, 1.0))
    first[...] = out[:HALO, :]
    last[...] = out[tile_rows - HALO:, :]


def lay_rows(slab, tile, above, below, cols):
    rows = tile.shape[0]
    tall = slab.shape[0]
    slab[:rows, :] = tile[:, cols]
    slab[rows:rows + HALO, :] = above[:, cols]
    slab[rows + HALO:tall - HALO, :] = jnp.zeros((tall - rows - 2 * HALO, 128), F32)
    slab[tall - HALO:, :] = below[:, cols]


def sides_kernel(tile, above, below, west, east, slab):
    cols = tile.shape[1]
    lanes = slab.shape[0] // 128
    for out, at, keep in ((west, 0, 0), (east, cols - 128, 128 - HALO)):
        lay_rows(slab, tile, above, below, slice(at, at + 128))
        for k in range(lanes):
            out[k] = slab[pl.ds(k, 128, stride=lanes), :].T[keep:keep + HALO, :]


def fill_kernel(
    tile, above, below, right, left, surface, depths, totals, slabs, turned, cells, keep, rate
):
    rows, cols = tile.shape
    quarters = cols // 128
    lanes, long, _ = turned.shape
    deep = long // 8

    for q in range(quarters):
        at = slice(q * 128, (q + 1) * 128)
        lay_rows(slabs.at[q], tile, above, below, at)
        for k in range(lanes):
            turned[k, at, :] = slabs[q, pl.ds(k, 128, stride=lanes), :].T
    for k in range(lanes):
        turned[k, cols:cols + HALO, :] = right[k]
        turned[k, cols + HALO:, :] = left[k]
    for v in range(deep):
        for k in range(lanes):
            values = turned[k, pl.ds(v, 8, stride=deep), :]
            unknown = values > 0.5 * GAP
            cells[v, k] = jnp.where(unknown, 0.0, values)
            keep[v, k] = jnp.where(unknown, 1.0 - 0.9, 1.0)
            rate[v, k] = jnp.where(unknown, 0.9 * 0.25, 0.0)

    def step(_, carry):
        opening = [cells[0, k] for k in range(lanes)]
        before = [pltpu.roll(cells[deep - 1, k], 1, axis=0) for k in range(lanes)]
        here = opening
        for v in range(deep):
            if v + 1 < deep:
                after = [cells[v + 1, k] for k in range(lanes)]
            else:
                after = [pltpu.roll(values, 7, axis=0) for values in opening]
            lower = [pltpu.roll(here[-1], 1, axis=1)] + here[:-1]
            upper = here[1:] + [pltpu.roll(here[0], 127, axis=1)]
            for k in range(lanes):
                total = (before[k] + after[k]) + (lower[k] + upper[k])
                cells[v, k] = keep[v, k] * here[k] + rate[v, k] * total
            before, here = here, after
        return carry

    lax.fori_loop(0, STEPS, step, 0)

    for v in range(deep):
        for k in range(lanes):
            turned[k, pl.ds(v, 8, stride=deep), :] = cells[v, k]
    for q in range(quarters):
        at = slice(q * 128, (q + 1) * 128)
        for k in range(lanes):
            slabs[q, pl.ds(k, 128, stride=lanes), :] = turned[k, at, :].T
        surface[:, at] = slabs[q, :rows, :]
    final = surface[...]
    soft = jnp.maximum(final, 0.0) + jnp.log1p(jnp.exp(-jnp.abs(final)))
    ahead = (iota((cols, cols), 0) < iota((cols, cols), 1)).astype(F32).astype(BF16)
    ones = jnp.ones((8, cols), BF16)
    south = jnp.zeros((rows, cols), F32)
    along = jnp.zeros((8, rows), F32)
    for term in reversed(split(soft)):
        south = south + jnp.dot(term, ahead, preferred_element_type=F32)
        along = along + lax.dot_general(
            ones, term, (((1,), (1,)), ((), ())), preferred_element_type=F32
        )
    whole = south[:, cols - 1:] + soft[:, cols - 1:]
    depths[0] = south
    depths[1] = (whole - south) - soft
    packed = jnp.where(iota((8, 128), 0) == 0, along[:, :128], along[:, 128:])
    for n in range(totals.shape[0]):
        totals[n] = packed


def light_kernel(place, extinction, side, depths, totals, out, carried):
    s = pl.program_id(0)
    _, rows, cols = depths.shape
    count = totals.shape[0]

    @pl.when(s == 0)
    def _():
        here = place[0]
        zero = jnp.zeros((8, 128), F32)
        for k in range(2):
            total = zero
            for n in range(count):
                counts = here < n if k else here > n
                total = total + jnp.where(counts, totals[n], zero)
            turned = jnp.concatenate([total, jnp.zeros((120, 128), F32)], axis=0).T
            for half in range(rows // 128):
                carried[k, half * 128:(half + 1) * 128, :] = jnp.broadcast_to(
                    turned[:, half:half + 1], (128, 128)
                )

    pick = side[s]
    rate = extinction[s] * (-1.4426950408889634 / (cols * count))
    for q in range(cols // 128):
        at = slice(q * 128, (q + 1) * 128)
        out[0, :, at] = jnp.exp2(rate * (depths[pick, :, at] + carried[pick]))


def moved(values, axis, hop):
    count = lax.axis_size(axis)
    return lax.ppermute(
        values, axis, [(i, i + hop) for i in range(count) if 0 <= i + hop < count]
    )


def body(heights, segment_ids, tile_owner, gap_mask, extinction, sun_side):
    rows_here = heights.shape[0]
    tile_rows, tile_cols = gap_mask.shape
    n_north = lax.axis_size("north")
    devices = lax.axis_size("east") * n_north
    chunks = rows_here // 128
    lanes = -(-(tile_rows + 2 * HALO) // 128)
    long = tile_cols + 2 * HALO
    mib = 1 << 20

    dealt = pl.pallas_call(
        deal_kernel,
        out_shape=jax.ShapeDtypeStruct((devices, BLOCK, 128), BF16),
        in_specs=[hbm()] * 3,
        out_specs=hbm(),
        scratch_shapes=[
            pltpu.VMEM((rows_here, 128), BF16),
            pltpu.VMEM((chunks, 128), I32),
            pltpu.VMEM((chunks, 128), I32),
            pltpu.VMEM((rows_here, 128), F32),
            pltpu.VMEM((devices * BLOCK, 128), F32),
            pltpu.VMEM((devices, BLOCK, 128), BF16),
            pltpu.VMEM((chunks, 128), I32),
            pltpu.VMEM((devices, 128), F32),
            pltpu.SMEM((chunks, 128), I32),
            pltpu.SemaphoreType.DMA((5 + PARTS,)),
        ],
        compiler_params=pltpu.CompilerParams(vmem_limit_bytes=60 * mib),
        name="deal",
    )(heights, tile_owner.reshape(chunks, 128), segment_ids.reshape(chunks, 128))

    got = lax.all_to_all(dealt, ("east", "north"), split_axis=0, concat_axis=0, tiled=True)

    strip = jax.ShapeDtypeStruct((HALO, tile_cols), F32)
    tile, first, last = pl.pallas_call(
        bin_kernel,
        out_shape=(jax.ShapeDtypeStruct((tile_rows, tile_cols), F32), strip, strip),
        in_specs=[vmem()] * 2,
        out_specs=(vmem(),) * 3,
        scratch_shapes=[
            pltpu.VMEM((tile_cols // 128, tile_rows, 256), F32),
            pltpu.VMEM((devices // 2, 128), F32),
            pltpu.VMEM((tile_cols // 128, devices // 2, 128), I32),
        ],
        compiler_params=pltpu.CompilerParams(vmem_limit_bytes=24 * mib),
        name="bin",
    )(got, gap_mask)

    below = moved(last, "east", 1)
    above = moved(first, "east", -1)

    turned = jax.ShapeDtypeStruct((lanes, HALO, 128), F32)
    west, east = pl.pallas_call(
        sides_kernel,
        out_shape=(turned, turned),
        in_specs=[vmem()] * 3,
        out_specs=(vmem(),) * 2,
        scratch_shapes=[pltpu.VMEM((lanes * 128, 128), F32)],
        compiler_params=pltpu.CompilerParams(vmem_limit_bytes=16 * mib),
        name="sides",
    )(tile, above, below)

    left = moved(east, "north", 1)
    right = moved(west, "north", -1)

    surface, depths, totals = pl.pallas_call(
        fill_kernel,
        out_shape=(
            jax.ShapeDtypeStruct((tile_rows, tile_cols), F32),
            jax.ShapeDtypeStruct((2, tile_rows, tile_cols), F32),
            jax.ShapeDtypeStruct((n_north, 8, 128), F32),
        ),
        in_specs=[vmem()] * 5,
        out_specs=(vmem(),) * 3,
        scratch_shapes=[
            pltpu.VMEM((tile_cols // 128, lanes * 128, 128), F32),
            pltpu.VMEM((lanes, long, 128), F32),
        ]
        + [pltpu.VMEM((long // 8, lanes, 8, 128), F32)] * 3,
        compiler_params=pltpu.CompilerParams(vmem_limit_bytes=32 * mib),
        name="fill",
    )(tile, above, below, right, left)

    totals = lax.all_to_all(totals, "north", split_axis=0, concat_axis=0, tiled=True)
    place = lax.axis_index("north").astype(I32).reshape(1)

    light = pl.pallas_call(
        light_kernel,
        grid=(NS,),
        out_shape=jax.ShapeDtypeStruct((NS, tile_rows, tile_cols), F32),
        in_specs=[smem()] * 3 + [vmem()] * 2,
        out_specs=pl.BlockSpec((1, tile_rows, tile_cols), lambda s: (s, 0, 0)),
        scratch_shapes=[pltpu.VMEM((2, tile_rows, 128), F32)],
        compiler_params=pltpu.CompilerParams(vmem_limit_bytes=24 * mib),
        name="light",
    )(place, extinction, sun_side, depths, totals)
    return surface, light


def solution(mesh):
    return jax.shard_map(
        body,
        mesh=mesh,
        in_specs=(
            P(("east", "north"), None),
            P(("east", "north")),
            P(("east", "north"), None),
            P("east", "north"),
            P(),
            P(),
        ),
        out_specs=(P("east", "north"), P(None, "east", "north")),
        check_vma=False,
    )
```

```python
import jax
import jax.numpy as jnp
from jax import lax
from jax.experimental import pallas as pl
from jax.experimental.pallas import tpu as pltpu
from jax.sharding import PartitionSpec as P

NS = 8
STEPS = 20
CAP = 64
BLOCK = 72
HALO = 24
GAP = 1000.0
GROUP = 64
TEAM = 8
DELAY = 2
PARTS = 4
PIECES = 1

F32 = jnp.float32
BF16 = jnp.bfloat16
I32 = jnp.int32


def vmem():
    return pl.BlockSpec(memory_space=pltpu.VMEM)


def hbm():
    return pl.BlockSpec(memory_space=pltpu.HBM)


def smem():
    return pl.BlockSpec(memory_space=pltpu.SMEM)


def iota(shape, dim):
    return lax.broadcasted_iota(I32, shape, dim)


def split(values):
    terms = []
    for _ in range(3):
        term = values.astype(BF16)
        terms.append(term)
        values = values - term.astype(F32)
    return terms


def deal_kernel(
    heights_in,
    owner_in,
    segment_in,
    out,
    heights,
    owner,
    segment,
    wide,
    dealt,
    packed,
    slots,
    ids,
    slots_s,
    sems,
):
    devices = out.shape[0]
    rows = heights.shape[0]
    chunks = rows // 128
    groups = chunks // TEAM
    loads = [
        pltpu.make_async_copy(src, dst, sems.at[i])
        for i, (src, dst) in enumerate(
            ((owner_in, owner), (segment_in, segment), (heights_in, heights))
        )
    ]
    for load in loads:
        load.start()
    zeros = jnp.zeros((BLOCK, 128), F32)

    @pl.loop(0, devices, unroll=4)
    def _(t):
        dealt[pl.ds(pl.multiple_of(t * BLOCK, 8), BLOCK), :] = zeros

    tile = iota((devices, 128), 0)
    before = (iota((128, 256), 0) < iota((128, 256), 1)).astype(F32).astype(BF16)
    place = iota((128, 128), 0) & (CAP - 1)
    loads[0].wait()
    loads[1].wait()

    def rank_team(g, carry):
        seen, named = carry
        for i in range(TEAM):
            c = g * TEAM + i
            own = owner[pl.ds(c, 1), :]
            hit = tile == own
            counts = jnp.dot(hit.astype(F32).astype(BF16), before, preferred_element_type=F32)
            rank = jnp.sum(jnp.where(hit, counts[:, :128] + seen, 0.0), axis=0, keepdims=True)
            rank = rank.astype(I32)
            slots[g, i:i + 1, :] = own * BLOCK + rank
            seg = segment[pl.ds(c, 1), :]
            code = (((seg & 127) + 128) << (seg >> 7)).astype(F32)
            coded = jnp.where(hit, jnp.broadcast_to(code, hit.shape), 0.0).astype(BF16)
            ranked = (place == rank).astype(F32).astype(BF16)
            named = named + lax.dot_general(
                coded, ranked, (((1,), (1,)), ((), ())), preferred_element_type=F32
            )
            seen = seen + counts[:, 128:]
        return seen, named

    def copy_slots(g):
        return pltpu.make_async_copy(slots.at[g], slots_s.at[g], sems.at[3 + lax.rem(g, DELAY)])

    def place_team(g):
        for i in range(TEAM):
            for j in range(128):
                row = g * (TEAM * 128) + (i * 128 + j)
                dealt[pl.ds(slots_s[g, i, j], 1), :] = wide[pl.ds(row, 1), :]

    start = jnp.zeros((devices, 128), F32)
    carry = start, start
    for g in range(DELAY):
        carry = rank_team(g, carry)
        copy_slots(g).start()
    loads[2].wait()

    @pl.loop(0, rows // 64, unroll=4)
    def _(c):
        at = pl.ds(pl.multiple_of(c * 64, 64), 64)
        wide[at, :] = heights[at, :].astype(F32)

    def overlap(g, carry):
        copy_slots(g - DELAY).wait()
        place_team(g - DELAY)
        carry = rank_team(g, carry)
        copy_slots(g).start()
        return carry

    _, named = lax.fori_loop(DELAY, groups, overlap, carry)
    ids[...] = named

    @pl.loop(0, devices, unroll=8)
    def _(t):
        dealt[pl.ds(t * BLOCK + CAP, 1), :] = ids[pl.ds(t, 1), :]

    for g in range(groups - DELAY, groups):
        copy_slots(g).wait()
        place_team(g)

    part = devices // PARTS
    stores = []
    for i in range(PARTS):

        @pl.loop(i * part, (i + 1) * part, unroll=4)
        def _(t):
            packed[t] = dealt[pl.ds(pl.multiple_of(t * BLOCK, 8), BLOCK), :].astype(BF16)

        at = pl.ds(i * part, part)
        stores.append(pltpu.make_async_copy(packed.at[at], out.at[at], sems.at[3 + DELAY + i]))
        stores[-1].start()
    for store in stores:
        store.wait()


def bin_kernel(got, gap_mask, out, one, two, acc, codes, lines):
    devices = got.shape[0]
    tile_rows, tile_cols = gap_mask.shape
    quarters = tile_cols // 128
    pairs = devices // 2
    low = iota((1, 128), 1) < CAP
    for p in range(pairs):
        a = got[2 * p][CAP:CAP + 1, :].astype(F32)
        b = got[2 * p + 1][CAP:CAP + 1, :].astype(F32)
        codes[p:p + 1, :] = jnp.where(low, a, b)
    code = codes[...]
    shift = jnp.zeros(code.shape, I32)
    for j in range(1, 8):
        shift = shift + (code >= 128.0 * 2**j).astype(I32)
    seg = (shift << 7) + (code.astype(I32) >> shift) - 128
    for q in range(quarters):
        lines[q] = jnp.where((code > 0.0) & ((seg & (quarters - 1)) == q), seg // quarters, -1)
    line = iota((tile_rows, 128), 0)
    ones = jnp.ones((GROUP * CAP, 128), BF16)

    def group(i, fresh):
        cells = jnp.concatenate([got[GROUP * i + j][:CAP, :] for j in range(GROUP)], axis=0)
        cells = jnp.concatenate([cells, ones], axis=1)
        for q in range(quarters):
            hot = jnp.concatenate(
                [
                    (line == lines[q, pl.ds(GROUP // 2 * i + j, 1), :]).astype(F32).astype(BF16)
                    for j in range(GROUP // 2)
                ],
                axis=1,
            )
            part = jnp.dot(hot, cells, preferred_element_type=F32)
            acc[q] = part if fresh else acc[q] + part

    group(0, True)

    @pl.loop(1, devices // GROUP)
    def _(i):
        group(i, False)

    for q in range(quarters):
        cols = slice(q * 128, (q + 1) * 128)
        total = acc[q]
        summed, counted = total[:, :128], total[:, 128:]
        unknown = (gap_mask[:, cols] == 1) | (counted == 0.0)
        out[:, cols] = jnp.where(unknown, GAP, summed / jnp.maximum(counted, 1.0))
    odd = lax.axis_index("east") % 2 == 1
    first, last = out[:HALO, :], out[tile_rows - HALO:, :]
    one[...] = jnp.where(odd, last, first)
    two[...] = jnp.where(odd, first, last)


def lay_rows(slab, tile, above, below, cols):
    rows = tile.shape[0]
    tall = slab.shape[0]
    slab[:rows, :] = tile[:, cols]
    slab[rows:rows + HALO, :] = above[:, cols]
    slab[rows + HALO:tall - HALO, :] = jnp.zeros((tall - rows - 2 * HALO, 128), F32)
    slab[tall - HALO:, :] = below[:, cols]


def upper_lower(axis, one, two):
    odd = lax.axis_index(axis) % 2 == 1
    return jnp.where(odd, one, two), jnp.where(odd, two, one)


def sides_kernel(tile, got_one, got_two, one, two, slab):
    cols = tile.shape[1]
    lanes = slab.shape[0] // 128
    above, below = upper_lower("east", got_one[...], got_two[...])
    odd = lax.axis_index("north") % 2 == 1
    strips = []
    for at, keep in ((0, 0), (cols - 128, 128 - HALO)):
        lay_rows(slab, tile, above, below, slice(at, at + 128))
        strips.append(
            [
                slab[pl.ds(k, 128, stride=lanes), :].T[keep:keep + HALO, :]
                for k in range(lanes)
            ]
        )
    for k in range(lanes):
        west, east = strips[0][k], strips[1][k]
        one[k] = jnp.where(odd, east, west)
        two[k] = jnp.where(odd, west, east)


def fill_kernel(
    tile,
    east_one,
    east_two,
    north_one,
    north_two,
    surface_out,
    depths,
    totals,
    surface,
    slabs,
    turned,
    cells,
    keep,
    rate,
    sem,
):
    rows, cols = tile.shape
    above, below = upper_lower("east", east_one[...], east_two[...])
    right, left = upper_lower("north", north_one[...], north_two[...])
    quarters = cols // 128
    lanes, long, _ = turned.shape
    deep = long // 8

    for q in range(quarters):
        at = slice(q * 128, (q + 1) * 128)
        lay_rows(slabs.at[q], tile, above, below, at)
        for k in range(lanes):
            turned[k, at, :] = slabs[q, pl.ds(k, 128, stride=lanes), :].T
    for k in range(lanes):
        turned[k, cols:cols + HALO, :] = right[k]
        turned[k, cols + HALO:, :] = left[k]
    for v in range(deep):
        for k in range(lanes):
            values = turned[k, pl.ds(v, 8, stride=deep), :]
            unknown = values > 0.5 * GAP
            cells[v, k] = jnp.where(unknown, 0.0, values)
            keep[v, k] = jnp.where(unknown, 1.0 - 0.9, 1.0)
            rate[v, k] = jnp.where(unknown, 0.9 * 0.25, 0.0)

    def step(_, carry):
        opening = [cells[0, k] for k in range(lanes)]
        before = [pltpu.roll(cells[deep - 1, k], 1, axis=0) for k in range(lanes)]
        here = opening
        for v in range(deep):
            if v + 1 < deep:
                after = [cells[v + 1, k] for k in range(lanes)]
            else:
                after = [pltpu.roll(values, 7, axis=0) for values in opening]
            lower = [pltpu.roll(here[-1], 1, axis=1)] + here[:-1]
            upper = here[1:] + [pltpu.roll(here[0], 127, axis=1)]
            for k in range(lanes):
                total = (before[k] + after[k]) + (lower[k] + upper[k])
                cells[v, k] = keep[v, k] * here[k] + rate[v, k] * total
            before, here = here, after
        return carry

    lax.fori_loop(0, STEPS, step, 0)

    for v in range(deep):
        for k in range(lanes):
            turned[k, pl.ds(v, 8, stride=deep), :] = cells[v, k]
    for q in range(quarters):
        at = slice(q * 128, (q + 1) * 128)
        for k in range(lanes):
            slabs[q, pl.ds(k, 128, stride=lanes), :] = turned[k, at, :].T
        surface[:, at] = slabs[q, :rows, :]
    store = pltpu.make_async_copy(surface, surface_out, sem)
    store.start()
    final = surface[...]
    soft = jnp.maximum(final, 0.0) + jnp.log1p(jnp.exp(-jnp.abs(final)))
    ahead = (iota((cols, cols), 0) < iota((cols, cols), 1)).astype(F32).astype(BF16)
    ones = jnp.ones((8, cols), BF16)
    south = jnp.zeros((rows, cols), F32)
    along = jnp.zeros((8, rows), F32)
    for term in reversed(split(soft)):
        south = south + jnp.dot(term, ahead, preferred_element_type=F32)
        along = along + lax.dot_general(
            ones, term, (((1,), (1,)), ((), ())), preferred_element_type=F32
        )
    whole = south[:, cols - 1:] + soft[:, cols - 1:]
    depths[0] = south
    depths[1] = (whole - south) - soft
    packed = jnp.where(iota((8, 128), 0) == 0, along[:, :128], along[:, 128:])
    for n in range(totals.shape[0]):
        totals[n] = packed
    store.wait()


def light_kernel(extinction, side, depths, totals, out, light, carried, sems):
    count, rows, cols = light.shape
    n_north = totals.shape[0]
    here = lax.axis_index("north")
    zero = jnp.zeros((8, 128), F32)
    for k in range(2):
        total = zero
        for n in range(n_north):
            counts = here < n if k else here > n
            total = total + jnp.where(counts, totals[n], zero)
        turned = jnp.concatenate([total, jnp.zeros((120, 128), F32)], axis=0).T
        for half in range(rows // 128):
            carried[k, half * 128:(half + 1) * 128, :] = jnp.broadcast_to(
                turned[:, half:half + 1], (128, 128)
            )

    def store(s, i):
        at = pl.ds(i * (rows // PIECES), rows // PIECES)
        return pltpu.make_async_copy(light.at[s, at], out.at[s, at], sems.at[s, i])

    @pl.loop(0, count)
    def _(s):
        pick = side[s]
        rate = extinction[s] * (-1.4426950408889634 / (cols * n_north))
        for i in range(PIECES):
            tall = slice(i * (rows // PIECES), (i + 1) * (rows // PIECES))
            for q in range(cols // 128):
                at = slice(q * 128, (q + 1) * 128)
                light[s, tall, at] = jnp.exp2(
                    rate * (depths[pick, tall, at] + carried[pick, tall, :])
                )
            store(s, i).start()

    @pl.loop(0, count)
    def _(s):
        for i in range(PIECES):
            store(s, i).wait()


def swapped(values, axis, start):
    count = lax.axis_size(axis)
    edges = [(i, i + 1) for i in range(start, count - 1, 2)]
    return lax.ppermute(values, axis, edges + [(j, i) for i, j in edges])


def body(heights, segment_ids, tile_owner, gap_mask, extinction, sun_side):
    rows_here = heights.shape[0]
    tile_rows, tile_cols = gap_mask.shape
    n_north = lax.axis_size("north")
    devices = lax.axis_size("east") * n_north
    chunks = rows_here // 128
    lanes = -(-(tile_rows + 2 * HALO) // 128)
    long = tile_cols + 2 * HALO
    mib = 1 << 20

    dealt = pl.pallas_call(
        deal_kernel,
        out_shape=jax.ShapeDtypeStruct((devices, BLOCK, 128), BF16),
        in_specs=[hbm()] * 3,
        out_specs=hbm(),
        scratch_shapes=[
            pltpu.VMEM((rows_here, 128), BF16),
            pltpu.VMEM((chunks, 128), I32),
            pltpu.VMEM((chunks, 128), I32),
            pltpu.VMEM((rows_here, 128), F32),
            pltpu.VMEM((devices * BLOCK, 128), F32),
            pltpu.VMEM((devices, BLOCK, 128), BF16),
            pltpu.VMEM((chunks // TEAM, 8, 128), I32),
            pltpu.VMEM((devices, 128), F32),
            pltpu.SMEM((chunks // TEAM, 8, 128), I32),
            pltpu.SemaphoreType.DMA((3 + DELAY + PARTS,)),
        ],
        compiler_params=pltpu.CompilerParams(vmem_limit_bytes=60 * mib),
        name="deal",
    )(heights, tile_owner.reshape(chunks, 128), segment_ids.reshape(chunks, 128))

    got = lax.all_to_all(dealt, ("east", "north"), split_axis=0, concat_axis=0, tiled=True)

    strip = jax.ShapeDtypeStruct((HALO, tile_cols), F32)
    tile, one, two = pl.pallas_call(
        bin_kernel,
        out_shape=(jax.ShapeDtypeStruct((tile_rows, tile_cols), F32), strip, strip),
        in_specs=[vmem()] * 2,
        out_specs=(vmem(),) * 3,
        scratch_shapes=[
            pltpu.VMEM((tile_cols // 128, tile_rows, 256), F32),
            pltpu.VMEM((devices // 2, 128), F32),
            pltpu.VMEM((tile_cols // 128, devices // 2, 128), I32),
        ],
        compiler_params=pltpu.CompilerParams(vmem_limit_bytes=24 * mib),
        name="bin",
    )(got, gap_mask)

    east = swapped(one, "east", 1), swapped(two, "east", 0)

    turned = jax.ShapeDtypeStruct((lanes, HALO, 128), F32)
    one, two = pl.pallas_call(
        sides_kernel,
        out_shape=(turned, turned),
        in_specs=[vmem()] * 3,
        out_specs=(vmem(),) * 2,
        scratch_shapes=[pltpu.VMEM((lanes * 128, 128), F32)],
        compiler_params=pltpu.CompilerParams(vmem_limit_bytes=16 * mib),
        name="sides",
    )(tile, *east)

    north = swapped(one, "north", 1), swapped(two, "north", 0)

    surface, depths, totals = pl.pallas_call(
        fill_kernel,
        out_shape=(
            jax.ShapeDtypeStruct((tile_rows, tile_cols), F32),
            jax.ShapeDtypeStruct((2, tile_rows, tile_cols), F32),
            jax.ShapeDtypeStruct((n_north, 8, 128), F32),
        ),
        in_specs=[vmem()] * 5,
        out_specs=(hbm(), vmem(), vmem()),
        scratch_shapes=[
            pltpu.VMEM((tile_rows, tile_cols), F32),
            pltpu.VMEM((tile_cols // 128, lanes * 128, 128), F32),
            pltpu.VMEM((lanes, long, 128), F32),
        ]
        + [pltpu.VMEM((long // 8, lanes, 8, 128), F32)] * 3
        + [pltpu.SemaphoreType.DMA],
        compiler_params=pltpu.CompilerParams(vmem_limit_bytes=32 * mib),
        name="fill",
    )(tile, *east, *north)

    totals = lax.all_to_all(totals, "north", split_axis=0, concat_axis=0, tiled=True)
    light = pl.pallas_call(
        light_kernel,
        out_shape=jax.ShapeDtypeStruct((NS, tile_rows, tile_cols), F32),
        in_specs=[smem()] * 2 + [vmem()] * 2,
        out_specs=hbm(),
        scratch_shapes=[
            pltpu.VMEM((NS, tile_rows, tile_cols), F32),
            pltpu.VMEM((2, tile_rows, 128), F32),
            pltpu.SemaphoreType.DMA((NS, PIECES)),
        ],
        compiler_params=pltpu.CompilerParams(vmem_limit_bytes=24 * mib),
        name="light",
    )(extinction, sun_side, depths, totals)
    return surface, light


def solution(mesh):
    return jax.shard_map(
        body,
        mesh=mesh,
        in_specs=(
            P(("east", "north"), None),
            P(("east", "north")),
            P(("east", "north"), None),
            P("east", "north"),
            P(),
            P(),
        ),
        out_specs=(P("east", "north"), P(None, "east", "north")),
        check_vma=False,
    )
```

```python
import jax
import jax.numpy as jnp
from jax import lax
from jax.experimental import pallas as pl
from jax.experimental.pallas import tpu as pltpu
from jax.sharding import PartitionSpec as P

NS = 8
STEPS = 20
CAP = 64
BLOCK = 72
HALO = 24
GAP = 1000.0
GROUP = 64
TEAM = 8
DELAY = 2
PARTS = 4
PIECES = 1

F32 = jnp.float32
BF16 = jnp.bfloat16
I32 = jnp.int32


def vmem():
    return pl.BlockSpec(memory_space=pltpu.VMEM)


def hbm():
    return pl.BlockSpec(memory_space=pltpu.HBM)


def smem():
    return pl.BlockSpec(memory_space=pltpu.SMEM)


def iota(shape, dim):
    return lax.broadcasted_iota(I32, shape, dim)


def split(values):
    terms = []
    for _ in range(3):
        term = values.astype(BF16)
        terms.append(term)
        values = values - term.astype(F32)
    return terms


def softplus(values):
    return jnp.maximum(values, 0.0) + jnp.log1p(jnp.exp(-jnp.abs(values)))


def deal_kernel(
    heights_in,
    owner_in,
    segment_in,
    out,
    heights,
    owner,
    segment,
    wide,
    dealt,
    packed,
    slots,
    ids,
    slots_s,
    sems,
):
    devices = out.shape[0]
    rows = heights.shape[0]
    chunks = rows // 128
    groups = chunks // TEAM
    loads = [
        pltpu.make_async_copy(src, dst, sems.at[i])
        for i, (src, dst) in enumerate(
            ((owner_in, owner), (segment_in, segment), (heights_in, heights))
        )
    ]
    for load in loads:
        load.start()
    zeros = jnp.zeros((BLOCK, 128), F32)

    @pl.loop(0, devices, unroll=4)
    def _(t):
        dealt[pl.ds(pl.multiple_of(t * BLOCK, 8), BLOCK), :] = zeros

    tile = iota((devices, 128), 0)
    before = (iota((128, 256), 0) < iota((128, 256), 1)).astype(F32).astype(BF16)
    place = iota((128, 128), 0) & (CAP - 1)
    loads[0].wait()
    loads[1].wait()

    def rank_team(g, carry):
        seen, named = carry
        for i in range(TEAM):
            c = g * TEAM + i
            own = owner[pl.ds(c, 1), :]
            hit = tile == own
            counts = jnp.dot(hit.astype(F32).astype(BF16), before, preferred_element_type=F32)
            rank = jnp.sum(jnp.where(hit, counts[:, :128] + seen, 0.0), axis=0, keepdims=True)
            rank = rank.astype(I32)
            slots[g, i:i + 1, :] = own * BLOCK + rank
            seg = segment[pl.ds(c, 1), :]
            code = (((seg & 127) + 128) << (seg >> 7)).astype(F32)
            coded = jnp.where(hit, jnp.broadcast_to(code, hit.shape), 0.0).astype(BF16)
            ranked = (place == rank).astype(F32).astype(BF16)
            named = named + lax.dot_general(
                coded, ranked, (((1,), (1,)), ((), ())), preferred_element_type=F32
            )
            seen = seen + counts[:, 128:]
        return seen, named

    def copy_slots(g):
        return pltpu.make_async_copy(slots.at[g], slots_s.at[g], sems.at[3 + lax.rem(g, DELAY)])

    def place_team(g):
        for i in range(TEAM):
            for j in range(128):
                row = g * (TEAM * 128) + (i * 128 + j)
                dealt[pl.ds(slots_s[g, i, j], 1), :] = wide[pl.ds(row, 1), :]

    start = jnp.zeros((devices, 128), F32)
    carry = start, start
    for g in range(DELAY):
        carry = rank_team(g, carry)
        copy_slots(g).start()
    loads[2].wait()

    @pl.loop(0, rows // 64, unroll=4)
    def _(c):
        at = pl.ds(pl.multiple_of(c * 64, 64), 64)
        wide[at, :] = heights[at, :].astype(F32)

    def overlap(g, carry):
        copy_slots(g - DELAY).wait()
        place_team(g - DELAY)
        carry = rank_team(g, carry)
        copy_slots(g).start()
        return carry

    _, named = lax.fori_loop(DELAY, groups, overlap, carry)
    ids[...] = named

    @pl.loop(0, devices, unroll=8)
    def _(t):
        dealt[pl.ds(t * BLOCK + CAP, 1), :] = ids[pl.ds(t, 1), :]

    for g in range(groups - DELAY, groups):
        copy_slots(g).wait()
        place_team(g)

    part = devices // PARTS
    stores = []
    for i in range(PARTS):

        @pl.loop(i * part, (i + 1) * part, unroll=4)
        def _(t):
            packed[t] = dealt[pl.ds(pl.multiple_of(t * BLOCK, 8), BLOCK), :].astype(BF16)

        at = pl.ds(i * part, part)
        stores.append(pltpu.make_async_copy(packed.at[at], out.at[at], sems.at[3 + DELAY + i]))
        stores[-1].start()
    for store in stores:
        store.wait()


def bin_kernel(got, gap_mask, out, one, two, acc, codes, lines):
    devices = got.shape[0]
    tile_rows, tile_cols = gap_mask.shape
    quarters = tile_cols // 128
    pairs = devices // 2
    low = iota((1, 128), 1) < CAP
    for p in range(pairs):
        a = got[2 * p][CAP:CAP + 1, :].astype(F32)
        b = got[2 * p + 1][CAP:CAP + 1, :].astype(F32)
        codes[p:p + 1, :] = jnp.where(low, a, b)
    code = codes[...]
    shift = jnp.zeros(code.shape, I32)
    for j in range(1, 8):
        shift = shift + (code >= 128.0 * 2**j).astype(I32)
    seg = (shift << 7) + (code.astype(I32) >> shift) - 128
    for q in range(quarters):
        lines[q] = jnp.where((code > 0.0) & ((seg & (quarters - 1)) == q), seg // quarters, -1)
    line = iota((tile_rows, 128), 0)
    ones = jnp.ones((GROUP * CAP, 128), BF16)

    def group(i, fresh):
        cells = jnp.concatenate([got[GROUP * i + j][:CAP, :] for j in range(GROUP)], axis=0)
        cells = jnp.concatenate([cells, ones], axis=1)
        for q in range(quarters):
            hot = jnp.concatenate(
                [
                    (line == lines[q, pl.ds(GROUP // 2 * i + j, 1), :]).astype(F32).astype(BF16)
                    for j in range(GROUP // 2)
                ],
                axis=1,
            )
            part = jnp.dot(hot, cells, preferred_element_type=F32)
            acc[q] = part if fresh else acc[q] + part

    group(0, True)

    @pl.loop(1, devices // GROUP)
    def _(i):
        group(i, False)

    for q in range(quarters):
        cols = slice(q * 128, (q + 1) * 128)
        total = acc[q]
        summed, counted = total[:, :128], total[:, 128:]
        unknown = (gap_mask[:, cols] == 1) | (counted == 0.0)
        out[:, cols] = jnp.where(unknown, GAP, summed / jnp.maximum(counted, 1.0))
    odd = lax.axis_index("east") % 2 == 1
    first, last = out[:HALO, :], out[tile_rows - HALO:, :]
    one[...] = jnp.where(odd, last, first)
    two[...] = jnp.where(odd, first, last)


def lay_rows(slab, tile, above, below, cols):
    rows = tile.shape[0]
    tall = slab.shape[0]
    slab[:rows, :] = tile[:, cols]
    slab[rows:rows + HALO, :] = above[:, cols]
    slab[rows + HALO:tall - HALO, :] = jnp.zeros((tall - rows - 2 * HALO, 128), F32)
    slab[tall - HALO:, :] = below[:, cols]


def upper_lower(axis, one, two):
    odd = lax.axis_index(axis) % 2 == 1
    return jnp.where(odd, one, two), jnp.where(odd, two, one)


def sides_kernel(tile, got_one, got_two, one, two, slab):
    cols = tile.shape[1]
    lanes = slab.shape[0] // 128
    above, below = upper_lower("east", got_one[...], got_two[...])
    odd = lax.axis_index("north") % 2 == 1
    strips = []
    for at, keep in ((0, 0), (cols - 128, 128 - HALO)):
        lay_rows(slab, tile, above, below, slice(at, at + 128))
        strips.append(
            [
                slab[pl.ds(k, 128, stride=lanes), :].T[keep:keep + HALO, :]
                for k in range(lanes)
            ]
        )
    for k in range(lanes):
        west, east = strips[0][k], strips[1][k]
        one[k] = jnp.where(odd, east, west)
        two[k] = jnp.where(odd, west, east)


def fill_kernel(
    tile,
    east_one,
    east_two,
    north_one,
    north_two,
    cells,
    totals,
    slabs,
    turned,
    keep,
    rate,
):
    rows, cols = tile.shape
    above, below = upper_lower("east", east_one[...], east_two[...])
    right, left = upper_lower("north", north_one[...], north_two[...])
    quarters = cols // 128
    lanes, long, _ = turned.shape
    deep = long // 8

    for q in range(quarters):
        at = slice(q * 128, (q + 1) * 128)
        lay_rows(slabs.at[q], tile, above, below, at)
        for k in range(lanes):
            turned[k, at, :] = slabs[q, pl.ds(k, 128, stride=lanes), :].T
    for k in range(lanes):
        turned[k, cols:cols + HALO, :] = right[k]
        turned[k, cols + HALO:, :] = left[k]
    for v in range(deep):
        for k in range(lanes):
            values = turned[k, pl.ds(v, 8, stride=deep), :]
            unknown = values > 0.5 * GAP
            cells[v, k] = jnp.where(unknown, 0.0, values)
            keep[v, k] = jnp.where(unknown, 1.0 - 0.9, 1.0)
            rate[v, k] = jnp.where(unknown, 0.9 * 0.25, 0.0)

    def step(_, carry):
        opening = [cells[0, k] for k in range(lanes)]
        before = [pltpu.roll(cells[deep - 1, k], 1, axis=0) for k in range(lanes)]
        here = opening
        for v in range(deep):
            if v + 1 < deep:
                after = [cells[v + 1, k] for k in range(lanes)]
            else:
                after = [pltpu.roll(values, 7, axis=0) for values in opening]
            lower = [pltpu.roll(here[-1], 1, axis=1)] + here[:-1]
            upper = here[1:] + [pltpu.roll(here[0], 127, axis=1)]
            for k in range(lanes):
                total = (before[k] + after[k]) + (lower[k] + upper[k])
                cells[v, k] = keep[v, k] * here[k] + rate[v, k] * total
            before, here = here, after
        return carry

    lax.fori_loop(0, STEPS, step, 0)

    sums = [jnp.zeros((8, 128), F32) for _ in range(lanes)]
    for v in range(deep):
        inside = iota((8, 128), 0) * deep + v < cols
        for k in range(lanes):
            soft = softplus(cells[v, k])
            sums[k] = sums[k] + (soft if 7 * deep + v < cols else jnp.where(inside, soft, 0.0))
    packed = jnp.zeros((8, 128), F32)
    for k in range(lanes):
        total = jnp.sum(sums[k], axis=0, keepdims=True)
        packed = packed + jnp.where(iota((8, 128), 0) == k, total, 0.0)
    for n in range(totals.shape[0]):
        totals[n] = packed


def depth_kernel(cells, surface_out, depths, surface, slabs, turned, sem):
    rows, cols = surface.shape
    quarters = cols // 128
    lanes = turned.shape[0]
    deep = cells.shape[0]
    for v in range(deep):
        for k in range(lanes):
            turned[k, pl.ds(v, 8, stride=deep), :] = cells[v, k]
    for q in range(quarters):
        at = slice(q * 128, (q + 1) * 128)
        for k in range(lanes):
            slabs[q, pl.ds(k, 128, stride=lanes), :] = turned[k, at, :].T
        surface[:, at] = slabs[q, :rows, :]
    store = pltpu.make_async_copy(surface, surface_out, sem)
    store.start()
    soft = softplus(surface[...])
    ahead = (iota((cols, cols), 0) < iota((cols, cols), 1)).astype(F32).astype(BF16)
    south = jnp.zeros((rows, cols), F32)
    for term in reversed(split(soft)):
        south = south + jnp.dot(term, ahead, preferred_element_type=F32)
    whole = south[:, cols - 1:] + soft[:, cols - 1:]
    depths[0] = south
    depths[1] = (whole - south) - soft
    store.wait()


def light_kernel(extinction, side, depths, totals, out, light, carried, sems):
    count, rows, cols = light.shape
    n_north = totals.shape[0]
    lanes = carried.shape[1] // 128
    here = lax.axis_index("north")
    zero = jnp.zeros((8, 128), F32)
    for k in range(2):
        total = zero
        for n in range(n_north):
            counts = here < n if k else here > n
            total = total + jnp.where(counts, totals[n], zero)
        turned = jnp.concatenate([total, jnp.zeros((120, 128), F32)], axis=0).T
        for lane in range(lanes):
            carried[k, pl.ds(lane, 128, stride=lanes), :] = jnp.broadcast_to(
                turned[:, lane:lane + 1], (128, 128)
            )

    def store(s, i):
        at = pl.ds(i * (rows // PIECES), rows // PIECES)
        return pltpu.make_async_copy(light.at[s, at], out.at[s, at], sems.at[s, i])

    @pl.loop(0, count)
    def _(s):
        pick = side[s]
        rate = extinction[s] * (-1.4426950408889634 / (cols * n_north))
        for i in range(PIECES):
            tall = slice(i * (rows // PIECES), (i + 1) * (rows // PIECES))
            for q in range(cols // 128):
                at = slice(q * 128, (q + 1) * 128)
                light[s, tall, at] = jnp.exp2(
                    rate * (depths[pick, tall, at] + carried[pick, tall, :])
                )
            store(s, i).start()

    @pl.loop(0, count)
    def _(s):
        for i in range(PIECES):
            store(s, i).wait()


def swapped(values, axis, start):
    count = lax.axis_size(axis)
    edges = [(i, i + 1) for i in range(start, count - 1, 2)]
    return lax.ppermute(values, axis, edges + [(j, i) for i, j in edges])


def body(heights, segment_ids, tile_owner, gap_mask, extinction, sun_side):
    rows_here = heights.shape[0]
    tile_rows, tile_cols = gap_mask.shape
    n_north = lax.axis_size("north")
    devices = lax.axis_size("east") * n_north
    chunks = rows_here // 128
    lanes = -(-(tile_rows + 2 * HALO) // 128)
    long = tile_cols + 2 * HALO
    mib = 1 << 20

    dealt = pl.pallas_call(
        deal_kernel,
        out_shape=jax.ShapeDtypeStruct((devices, BLOCK, 128), BF16),
        in_specs=[hbm()] * 3,
        out_specs=hbm(),
        scratch_shapes=[
            pltpu.VMEM((rows_here, 128), BF16),
            pltpu.VMEM((chunks, 128), I32),
            pltpu.VMEM((chunks, 128), I32),
            pltpu.VMEM((rows_here, 128), F32),
            pltpu.VMEM((devices * BLOCK, 128), F32),
            pltpu.VMEM((devices, BLOCK, 128), BF16),
            pltpu.VMEM((chunks // TEAM, 8, 128), I32),
            pltpu.VMEM((devices, 128), F32),
            pltpu.SMEM((chunks // TEAM, 8, 128), I32),
            pltpu.SemaphoreType.DMA((3 + DELAY + PARTS,)),
        ],
        compiler_params=pltpu.CompilerParams(vmem_limit_bytes=60 * mib),
        name="deal",
    )(heights, tile_owner.reshape(chunks, 128), segment_ids.reshape(chunks, 128))

    got = lax.all_to_all(dealt, ("east", "north"), split_axis=0, concat_axis=0, tiled=True)

    strip = jax.ShapeDtypeStruct((HALO, tile_cols), F32)
    tile, one, two = pl.pallas_call(
        bin_kernel,
        out_shape=(jax.ShapeDtypeStruct((tile_rows, tile_cols), F32), strip, strip),
        in_specs=[vmem()] * 2,
        out_specs=(vmem(),) * 3,
        scratch_shapes=[
            pltpu.VMEM((tile_cols // 128, tile_rows, 256), F32),
            pltpu.VMEM((devices // 2, 128), F32),
            pltpu.VMEM((tile_cols // 128, devices // 2, 128), I32),
        ],
        compiler_params=pltpu.CompilerParams(vmem_limit_bytes=24 * mib),
        name="bin",
    )(got, gap_mask)

    east = swapped(one, "east", 1), swapped(two, "east", 0)

    turned = jax.ShapeDtypeStruct((lanes, HALO, 128), F32)
    one, two = pl.pallas_call(
        sides_kernel,
        out_shape=(turned, turned),
        in_specs=[vmem()] * 3,
        out_specs=(vmem(),) * 2,
        scratch_shapes=[pltpu.VMEM((lanes * 128, 128), F32)],
        compiler_params=pltpu.CompilerParams(vmem_limit_bytes=16 * mib),
        name="sides",
    )(tile, *east)

    north = swapped(one, "north", 1), swapped(two, "north", 0)

    shape = jax.ShapeDtypeStruct((long // 8, lanes, 8, 128), F32)
    cells, totals = pl.pallas_call(
        fill_kernel,
        out_shape=(shape, jax.ShapeDtypeStruct((n_north, 8, 128), F32)),
        in_specs=[vmem()] * 5,
        out_specs=(vmem(), vmem()),
        scratch_shapes=[
            pltpu.VMEM((tile_cols // 128, lanes * 128, 128), F32),
            pltpu.VMEM((lanes, long, 128), F32),
        ]
        + [pltpu.VMEM(shape.shape, F32)] * 2,
        compiler_params=pltpu.CompilerParams(vmem_limit_bytes=32 * mib),
        name="fill",
    )(tile, *east, *north)

    totals = lax.all_to_all(totals, "north", split_axis=0, concat_axis=0, tiled=True)

    surface, depths = pl.pallas_call(
        depth_kernel,
        out_shape=(
            jax.ShapeDtypeStruct((tile_rows, tile_cols), F32),
            jax.ShapeDtypeStruct((2, tile_rows, tile_cols), F32),
        ),
        in_specs=[vmem()],
        out_specs=(hbm(), vmem()),
        scratch_shapes=[
            pltpu.VMEM((tile_rows, tile_cols), F32),
            pltpu.VMEM((tile_cols // 128, lanes * 128, 128), F32),
            pltpu.VMEM((lanes, long, 128), F32),
            pltpu.SemaphoreType.DMA,
        ],
        compiler_params=pltpu.CompilerParams(vmem_limit_bytes=16 * mib),
        cost_estimate=pl.CostEstimate(
            flops=6 * tile_rows * tile_cols * tile_cols,
            bytes_accessed=16 * tile_rows * tile_cols,
            transcendentals=2 * tile_rows * tile_cols,
        ),
        name="depth",
    )(cells)

    light = pl.pallas_call(
        light_kernel,
        out_shape=jax.ShapeDtypeStruct((NS, tile_rows, tile_cols), F32),
        in_specs=[smem()] * 2 + [vmem()] * 2,
        out_specs=hbm(),
        scratch_shapes=[
            pltpu.VMEM((NS, tile_rows, tile_cols), F32),
            pltpu.VMEM((2, lanes * 128, 128), F32),
            pltpu.SemaphoreType.DMA((NS, PIECES)),
        ],
        compiler_params=pltpu.CompilerParams(vmem_limit_bytes=24 * mib),
        name="light",
    )(extinction, sun_side, depths, totals)
    return surface, light


def solution(mesh):
    return jax.shard_map(
        body,
        mesh=mesh,
        in_specs=(
            P(("east", "north"), None),
            P(("east", "north")),
            P(("east", "north"), None),
            P("east", "north"),
            P(),
            P(),
        ),
        out_specs=(P("east", "north"), P(None, "east", "north")),
        check_vma=False,
    )
```

```python
import jax
import jax.numpy as jnp
from jax import lax
from jax.experimental import pallas as pl
from jax.experimental.pallas import tpu as pltpu
from jax.sharding import PartitionSpec as P

NS = 8
STEPS = 20
CAP = 64
BLOCK = 72
HALO = 24
GAP = 1000.0
GROUP = 64
TEAM = 8
DELAY = 2
PARTS = 4
PIECES = 1

F32 = jnp.float32
BF16 = jnp.bfloat16
I32 = jnp.int32


def vmem():
    return pl.BlockSpec(memory_space=pltpu.VMEM)


def hbm():
    return pl.BlockSpec(memory_space=pltpu.HBM)


def smem():
    return pl.BlockSpec(memory_space=pltpu.SMEM)


def iota(shape, dim):
    return lax.broadcasted_iota(I32, shape, dim)


def split(values):
    terms = []
    for _ in range(3):
        term = values.astype(BF16)
        terms.append(term)
        values = values - term.astype(F32)
    return terms


def softplus(values):
    return jnp.log(1.0 + jnp.exp(values))


def deal_kernel(
    heights_in,
    owner_in,
    segment_in,
    out,
    heights,
    owner,
    segment,
    wide,
    dealt,
    packed,
    slots,
    ids,
    slots_s,
    sems,
):
    devices = out.shape[0]
    rows = heights.shape[0]
    chunks = rows // 128
    groups = chunks // TEAM
    loads = [
        pltpu.make_async_copy(src, dst, sems.at[i])
        for i, (src, dst) in enumerate(
            ((owner_in, owner), (segment_in, segment), (heights_in, heights))
        )
    ]
    for load in loads:
        load.start()
    zeros = jnp.zeros((BLOCK, 128), F32)

    @pl.loop(0, devices, unroll=4)
    def _(t):
        dealt[pl.ds(pl.multiple_of(t * BLOCK, 8), BLOCK), :] = zeros

    tile = iota((devices, 128), 0)
    before = (iota((128, 256), 0) < iota((128, 256), 1)).astype(F32).astype(BF16)
    place = iota((128, 128), 0) & (CAP - 1)
    loads[0].wait()
    loads[1].wait()

    def rank_team(g, carry):
        seen, named = carry
        for i in range(TEAM):
            c = g * TEAM + i
            own = owner[pl.ds(c, 1), :]
            hit = tile == own
            counts = jnp.dot(hit.astype(F32).astype(BF16), before, preferred_element_type=F32)
            rank = jnp.sum(jnp.where(hit, counts[:, :128] + seen, 0.0), axis=0, keepdims=True)
            rank = rank.astype(I32)
            slots[g, i:i + 1, :] = own * BLOCK + rank
            seg = segment[pl.ds(c, 1), :]
            code = (((seg & 127) + 128) << (seg >> 7)).astype(F32)
            coded = jnp.where(hit, jnp.broadcast_to(code, hit.shape), 0.0).astype(BF16)
            ranked = (place == rank).astype(F32).astype(BF16)
            named = named + lax.dot_general(
                coded, ranked, (((1,), (1,)), ((), ())), preferred_element_type=F32
            )
            seen = seen + counts[:, 128:]
        return seen, named

    def copy_slots(g):
        return pltpu.make_async_copy(slots.at[g], slots_s.at[g], sems.at[3 + lax.rem(g, DELAY)])

    def place_team(g):
        for i in range(TEAM):
            for j in range(128):
                row = g * (TEAM * 128) + (i * 128 + j)
                dealt[pl.ds(slots_s[g, i, j], 1), :] = wide[pl.ds(row, 1), :]

    start = jnp.zeros((devices, 128), F32)
    carry = start, start
    for g in range(DELAY):
        carry = rank_team(g, carry)
        copy_slots(g).start()
    loads[2].wait()

    @pl.loop(0, rows // 64, unroll=4)
    def _(c):
        at = pl.ds(pl.multiple_of(c * 64, 64), 64)
        wide[at, :] = heights[at, :].astype(F32)

    def overlap(g, carry):
        copy_slots(g - DELAY).wait()
        place_team(g - DELAY)
        carry = rank_team(g, carry)
        copy_slots(g).start()
        return carry

    _, named = lax.fori_loop(DELAY, groups, overlap, carry)
    ids[...] = named

    @pl.loop(0, devices, unroll=8)
    def _(t):
        dealt[pl.ds(t * BLOCK + CAP, 1), :] = ids[pl.ds(t, 1), :]

    for g in range(groups - DELAY, groups):
        copy_slots(g).wait()
        place_team(g)

    part = devices // PARTS
    stores = []
    for i in range(PARTS):

        @pl.loop(i * part, (i + 1) * part, unroll=4)
        def _(t):
            packed[t] = dealt[pl.ds(pl.multiple_of(t * BLOCK, 8), BLOCK), :].astype(BF16)

        at = pl.ds(i * part, part)
        stores.append(pltpu.make_async_copy(packed.at[at], out.at[at], sems.at[3 + DELAY + i]))
        stores[-1].start()
    for store in stores:
        store.wait()


def bin_kernel(got, gap_mask, out, one, two, acc, codes, lines):
    devices = got.shape[0]
    tile_rows, tile_cols = gap_mask.shape
    quarters = tile_cols // 128
    pairs = devices // 2
    low = iota((1, 128), 1) < CAP
    for p in range(pairs):
        a = got[2 * p][CAP:CAP + 1, :].astype(F32)
        b = got[2 * p + 1][CAP:CAP + 1, :].astype(F32)
        codes[p:p + 1, :] = jnp.where(low, a, b)
    code = codes[...]
    shift = jnp.zeros(code.shape, I32)
    for j in range(1, 8):
        shift = shift + (code >= 128.0 * 2**j).astype(I32)
    seg = (shift << 7) + (code.astype(I32) >> shift) - 128
    for q in range(quarters):
        lines[q] = jnp.where((code > 0.0) & ((seg & (quarters - 1)) == q), seg // quarters, -1)
    line = iota((tile_rows, 128), 0)
    ones = jnp.ones((GROUP * CAP, 128), BF16)

    def group(i, fresh):
        cells = jnp.concatenate([got[GROUP * i + j][:CAP, :] for j in range(GROUP)], axis=0)
        cells = jnp.concatenate([cells, ones], axis=1)
        for q in range(quarters):
            hot = jnp.concatenate(
                [
                    (line == lines[q, pl.ds(GROUP // 2 * i + j, 1), :]).astype(F32).astype(BF16)
                    for j in range(GROUP // 2)
                ],
                axis=1,
            )
            part = jnp.dot(hot, cells, preferred_element_type=F32)
            acc[q] = part if fresh else acc[q] + part

    group(0, True)

    @pl.loop(1, devices // GROUP)
    def _(i):
        group(i, False)

    for q in range(quarters):
        cols = slice(q * 128, (q + 1) * 128)
        total = acc[q]
        summed, counted = total[:, :128], total[:, 128:]
        unknown = (gap_mask[:, cols] == 1) | (counted == 0.0)
        out[:, cols] = jnp.where(unknown, GAP, summed / jnp.maximum(counted, 1.0))
    odd = lax.axis_index("east") % 2 == 1
    first, last = out[:HALO, :], out[tile_rows - HALO:, :]
    one[...] = jnp.where(odd, last, first)
    two[...] = jnp.where(odd, first, last)


def lay_rows(slab, tile, above, below, cols):
    rows = tile.shape[0]
    tall = slab.shape[0]
    slab[:rows, :] = tile[:, cols]
    slab[rows:rows + HALO, :] = above[:, cols]
    slab[rows + HALO:tall - HALO, :] = jnp.zeros((tall - rows - 2 * HALO, 128), F32)
    slab[tall - HALO:, :] = below[:, cols]


def upper_lower(axis, one, two):
    odd = lax.axis_index(axis) % 2 == 1
    return jnp.where(odd, one, two), jnp.where(odd, two, one)


def sides_kernel(tile, got_one, got_two, one, two, slab):
    cols = tile.shape[1]
    lanes = slab.shape[0] // 128
    above, below = upper_lower("east", got_one[...], got_two[...])
    odd = lax.axis_index("north") % 2 == 1
    strips = []
    for at, keep in ((0, 0), (cols - 128, 128 - HALO)):
        lay_rows(slab, tile, above, below, slice(at, at + 128))
        strips.append(
            [
                slab[pl.ds(k, 128, stride=lanes), :].T[keep:keep + HALO, :]
                for k in range(lanes)
            ]
        )
    for k in range(lanes):
        west, east = strips[0][k], strips[1][k]
        one[k] = jnp.where(odd, east, west)
        two[k] = jnp.where(odd, west, east)


def turn_kernel(tile, east_one, east_two, coded, slabs, turned):
    cols = tile.shape[1]
    deep, lanes, _, _ = coded.shape
    above, below = upper_lower("east", east_one[...], east_two[...])
    for q in range(cols // 128):
        at = slice(q * 128, (q + 1) * 128)
        lay_rows(slabs.at[q], tile, above, below, at)
        for k in range(lanes):
            turned[k, at, :] = slabs[q, pl.ds(k, 128, stride=lanes), :].T
    for k in range(lanes):
        turned[k, cols:, :] = jnp.zeros((2 * HALO, 128), F32)
    for v in range(deep):
        for k in range(lanes):
            coded[v, k] = turned[k, pl.ds(v, 8, stride=deep), :]


def fill_kernel(coded, north_one, north_two, cells, totals, halo, keep, rate):
    deep, lanes, _, _ = coded.shape
    long = 8 * deep
    cols = long - 2 * HALO
    right, left = upper_lower("north", north_one[...], north_two[...])
    for k in range(lanes):
        halo[k, cols:cols + HALO, :] = right[k]
        halo[k, cols + HALO:, :] = left[k]
    for v in range(deep):
        column = iota((8, 128), 0) * deep + v
        for k in range(lanes):
            values = coded[v, k]
            if 7 * deep + v >= cols:
                beyond = halo[k, pl.ds(v, 8, stride=deep), :]
                values = jnp.where(column >= cols, beyond, values)
            unknown = values > 0.5 * GAP
            cells[v, k] = jnp.where(unknown, 0.0, values)
            keep[v, k] = jnp.where(unknown, 1.0 - 0.9, 1.0)
            rate[v, k] = jnp.where(unknown, 0.9 * 0.25, 0.0)

    def step(_, carry):
        opening = [cells[0, k] for k in range(lanes)]
        before = [pltpu.roll(cells[deep - 1, k], 1, axis=0) for k in range(lanes)]
        here = opening
        for v in range(deep):
            if v + 1 < deep:
                after = [cells[v + 1, k] for k in range(lanes)]
            else:
                after = [pltpu.roll(values, 7, axis=0) for values in opening]
            lower = [pltpu.roll(here[-1], 1, axis=1)] + here[:-1]
            upper = here[1:] + [pltpu.roll(here[0], 127, axis=1)]
            for k in range(lanes):
                total = (before[k] + after[k]) + (lower[k] + upper[k])
                cells[v, k] = keep[v, k] * here[k] + rate[v, k] * total
            before, here = here, after
        return carry

    lax.fori_loop(0, STEPS, step, 0, unroll=2)

    sums = [jnp.zeros((8, 128), F32) for _ in range(lanes)]
    for v in range(deep):
        inside = iota((8, 128), 0) * deep + v < cols
        for k in range(lanes):
            soft = softplus(cells[v, k])
            sums[k] = sums[k] + (soft if 7 * deep + v < cols else jnp.where(inside, soft, 0.0))
    packed = jnp.zeros((8, 128), F32)
    for k in range(lanes):
        total = jnp.sum(sums[k], axis=0, keepdims=True)
        packed = packed + jnp.where(iota((8, 128), 0) == k, total, 0.0)
    for n in range(totals.shape[0]):
        totals[n] = packed


def depth_kernel(cells, surface_out, depths, surface, slabs, turned, sem):
    rows, cols = surface.shape
    quarters = cols // 128
    lanes = turned.shape[0]
    deep = cells.shape[0]
    for v in range(deep):
        for k in range(lanes):
            turned[k, pl.ds(v, 8, stride=deep), :] = cells[v, k]
    for q in range(quarters):
        at = slice(q * 128, (q + 1) * 128)
        for k in range(lanes):
            slabs[q, pl.ds(k, 128, stride=lanes), :] = turned[k, at, :].T
        surface[:, at] = slabs[q, :rows, :]
    store = pltpu.make_async_copy(surface, surface_out, sem)
    store.start()
    soft = softplus(surface[...])
    ahead = (iota((cols, cols), 0) < iota((cols, cols), 1)).astype(F32).astype(BF16)
    south = jnp.zeros((rows, cols), F32)
    for term in reversed(split(soft)):
        south = south + jnp.dot(term, ahead, preferred_element_type=F32)
    whole = south[:, cols - 1:] + soft[:, cols - 1:]
    depths[0] = south
    depths[1] = (whole - south) - soft
    store.wait()


def light_kernel(extinction, side, depths, totals, out, light, carried, sems):
    count, rows, cols = light.shape
    n_north = totals.shape[0]
    lanes = carried.shape[1] // 128
    here = lax.axis_index("north")
    zero = jnp.zeros((8, 128), F32)
    for k in range(2):
        total = zero
        for n in range(n_north):
            counts = here < n if k else here > n
            total = total + jnp.where(counts, totals[n], zero)
        turned = jnp.concatenate([total, jnp.zeros((120, 128), F32)], axis=0).T
        for lane in range(lanes):
            carried[k, pl.ds(lane, 128, stride=lanes), :] = jnp.broadcast_to(
                turned[:, lane:lane + 1], (128, 128)
            )

    def store(s, i):
        at = pl.ds(i * (rows // PIECES), rows // PIECES)
        return pltpu.make_async_copy(light.at[s, at], out.at[s, at], sems.at[s, i])

    @pl.loop(0, count)
    def _(s):
        pick = side[s]
        rate = extinction[s] * (-1.4426950408889634 / (cols * n_north))
        for i in range(PIECES):
            tall = slice(i * (rows // PIECES), (i + 1) * (rows // PIECES))
            for q in range(cols // 128):
                at = slice(q * 128, (q + 1) * 128)
                light[s, tall, at] = jnp.exp2(
                    rate * (depths[pick, tall, at] + carried[pick, tall, :])
                )
            store(s, i).start()

    @pl.loop(0, count)
    def _(s):
        for i in range(PIECES):
            store(s, i).wait()


def swapped(values, axis, start):
    count = lax.axis_size(axis)
    edges = [(i, i + 1) for i in range(start, count - 1, 2)]
    return lax.ppermute(values, axis, edges + [(j, i) for i, j in edges])


def body(heights, segment_ids, tile_owner, gap_mask, extinction, sun_side):
    rows_here = heights.shape[0]
    tile_rows, tile_cols = gap_mask.shape
    n_north = lax.axis_size("north")
    devices = lax.axis_size("east") * n_north
    chunks = rows_here // 128
    lanes = -(-(tile_rows + 2 * HALO) // 128)
    long = tile_cols + 2 * HALO
    mib = 1 << 20

    dealt = pl.pallas_call(
        deal_kernel,
        out_shape=jax.ShapeDtypeStruct((devices, BLOCK, 128), BF16),
        in_specs=[hbm()] * 3,
        out_specs=hbm(),
        scratch_shapes=[
            pltpu.VMEM((rows_here, 128), BF16),
            pltpu.VMEM((chunks, 128), I32),
            pltpu.VMEM((chunks, 128), I32),
            pltpu.VMEM((rows_here, 128), F32),
            pltpu.VMEM((devices * BLOCK, 128), F32),
            pltpu.VMEM((devices, BLOCK, 128), BF16),
            pltpu.VMEM((chunks // TEAM, 8, 128), I32),
            pltpu.VMEM((devices, 128), F32),
            pltpu.SMEM((chunks // TEAM, 8, 128), I32),
            pltpu.SemaphoreType.DMA((3 + DELAY + PARTS,)),
        ],
        compiler_params=pltpu.CompilerParams(vmem_limit_bytes=60 * mib),
        name="deal",
    )(heights, tile_owner.reshape(chunks, 128), segment_ids.reshape(chunks, 128))

    got = lax.all_to_all(dealt, ("east", "north"), split_axis=0, concat_axis=0, tiled=True)

    strip = jax.ShapeDtypeStruct((HALO, tile_cols), F32)
    tile, one, two = pl.pallas_call(
        bin_kernel,
        out_shape=(jax.ShapeDtypeStruct((tile_rows, tile_cols), F32), strip, strip),
        in_specs=[vmem()] * 2,
        out_specs=(vmem(),) * 3,
        scratch_shapes=[
            pltpu.VMEM((tile_cols // 128, tile_rows, 256), F32),
            pltpu.VMEM((devices // 2, 128), F32),
            pltpu.VMEM((tile_cols // 128, devices // 2, 128), I32),
        ],
        compiler_params=pltpu.CompilerParams(vmem_limit_bytes=24 * mib),
        name="bin",
    )(got, gap_mask)

    east = swapped(one, "east", 1), swapped(two, "east", 0)

    turned = jax.ShapeDtypeStruct((lanes, HALO, 128), F32)
    one, two = pl.pallas_call(
        sides_kernel,
        out_shape=(turned, turned),
        in_specs=[vmem()] * 3,
        out_specs=(vmem(),) * 2,
        scratch_shapes=[pltpu.VMEM((lanes * 128, 128), F32)],
        compiler_params=pltpu.CompilerParams(vmem_limit_bytes=16 * mib),
        name="sides",
    )(tile, *east)

    north = swapped(one, "north", 1), swapped(two, "north", 0)

    shape = jax.ShapeDtypeStruct((long // 8, lanes, 8, 128), F32)
    coded = pl.pallas_call(
        turn_kernel,
        out_shape=shape,
        in_specs=[vmem()] * 3,
        out_specs=vmem(),
        scratch_shapes=[
            pltpu.VMEM((tile_cols // 128, lanes * 128, 128), F32),
            pltpu.VMEM((lanes, long, 128), F32),
        ],
        compiler_params=pltpu.CompilerParams(vmem_limit_bytes=16 * mib),
        cost_estimate=pl.CostEstimate(
            flops=4 * tile_rows * tile_cols,
            bytes_accessed=16 * tile_rows * tile_cols,
            transcendentals=0,
        ),
        name="turn",
    )(tile, *east)

    cells, totals = pl.pallas_call(
        fill_kernel,
        out_shape=(shape, jax.ShapeDtypeStruct((n_north, 8, 128), F32)),
        in_specs=[vmem()] * 3,
        out_specs=(vmem(), vmem()),
        scratch_shapes=[pltpu.VMEM((lanes, long, 128), F32)] + [pltpu.VMEM(shape.shape, F32)] * 2,
        compiler_params=pltpu.CompilerParams(vmem_limit_bytes=32 * mib),
        name="fill",
    )(coded, *north)

    totals = lax.all_to_all(totals, "north", split_axis=0, concat_axis=0, tiled=True)

    surface, depths = pl.pallas_call(
        depth_kernel,
        out_shape=(
            jax.ShapeDtypeStruct((tile_rows, tile_cols), F32),
            jax.ShapeDtypeStruct((2, tile_rows, tile_cols), F32),
        ),
        in_specs=[vmem()],
        out_specs=(hbm(), vmem()),
        scratch_shapes=[
            pltpu.VMEM((tile_rows, tile_cols), F32),
            pltpu.VMEM((tile_cols // 128, lanes * 128, 128), F32),
            pltpu.VMEM((lanes, long, 128), F32),
            pltpu.SemaphoreType.DMA,
        ],
        compiler_params=pltpu.CompilerParams(vmem_limit_bytes=16 * mib),
        cost_estimate=pl.CostEstimate(
            flops=6 * tile_rows * tile_cols * tile_cols,
            bytes_accessed=16 * tile_rows * tile_cols,
            transcendentals=2 * tile_rows * tile_cols,
        ),
        name="depth",
    )(cells)

    light = pl.pallas_call(
        light_kernel,
        out_shape=jax.ShapeDtypeStruct((NS, tile_rows, tile_cols), F32),
        in_specs=[smem()] * 2 + [vmem()] * 2,
        out_specs=hbm(),
        scratch_shapes=[
            pltpu.VMEM((NS, tile_rows, tile_cols), F32),
            pltpu.VMEM((2, lanes * 128, 128), F32),
            pltpu.SemaphoreType.DMA((NS, PIECES)),
        ],
        compiler_params=pltpu.CompilerParams(vmem_limit_bytes=24 * mib),
        name="light",
    )(extinction, sun_side, depths, totals)
    return surface, light


def solution(mesh):
    return jax.shard_map(
        body,
        mesh=mesh,
        in_specs=(
            P(("east", "north"), None),
            P(("east", "north")),
            P(("east", "north"), None),
            P("east", "north"),
            P(),
            P(),
        ),
        out_specs=(P("east", "north"), P(None, "east", "north")),
        check_vma=False,
    )
```

```python
import jax
import jax.numpy as jnp
from jax import lax
from jax.experimental import pallas as pl
from jax.experimental.pallas import tpu as pltpu
from jax.sharding import PartitionSpec as P

NS = 8
STEPS = 20
CAP = 64
BLOCK = 72
HALO = 24
GAP = 1000.0
GROUP = 64
TEAM = 8
DELAY = 2
PARTS = 4
PIECES = 1

F32 = jnp.float32
BF16 = jnp.bfloat16
I32 = jnp.int32


def vmem():
    return pl.BlockSpec(memory_space=pltpu.VMEM)


def hbm():
    return pl.BlockSpec(memory_space=pltpu.HBM)


def smem():
    return pl.BlockSpec(memory_space=pltpu.SMEM)


def iota(shape, dim):
    return lax.broadcasted_iota(I32, shape, dim)


def split(values):
    terms = []
    for _ in range(3):
        term = values.astype(BF16)
        terms.append(term)
        values = values - term.astype(F32)
    return terms


def softplus(values):
    return jnp.log(1.0 + jnp.exp(values))


def deal_kernel(
    heights_in,
    owner_in,
    segment_in,
    out,
    heights,
    owner,
    segment,
    wide,
    dealt,
    packed,
    slots,
    ids,
    slots_s,
    sems,
):
    devices = out.shape[0]
    rows = heights.shape[0]
    chunks = rows // 128
    groups = chunks // TEAM
    loads = [
        pltpu.make_async_copy(src, dst, sems.at[i])
        for i, (src, dst) in enumerate(
            ((owner_in, owner), (segment_in, segment), (heights_in, heights))
        )
    ]
    for load in loads:
        load.start()
    zeros = jnp.zeros((BLOCK, 128), F32)

    @pl.loop(0, devices, unroll=4)
    def _(t):
        dealt[pl.ds(pl.multiple_of(t * BLOCK, 8), BLOCK), :] = zeros

    tile = iota((devices, 128), 0)
    before = (iota((128, 256), 0) < iota((128, 256), 1)).astype(F32).astype(BF16)
    place = iota((128, 128), 0) & (CAP - 1)
    loads[0].wait()
    loads[1].wait()

    def rank_team(g, carry):
        seen, named = carry
        for i in range(TEAM):
            c = g * TEAM + i
            own = owner[pl.ds(c, 1), :]
            hit = tile == own
            counts = jnp.dot(hit.astype(F32).astype(BF16), before, preferred_element_type=F32)
            rank = jnp.sum(jnp.where(hit, counts[:, :128] + seen, 0.0), axis=0, keepdims=True)
            rank = rank.astype(I32)
            slots[g, i:i + 1, :] = own * BLOCK + rank
            seg = segment[pl.ds(c, 1), :]
            code = (((seg & 127) + 128) << (seg >> 7)).astype(F32)
            coded = jnp.where(hit, jnp.broadcast_to(code, hit.shape), 0.0).astype(BF16)
            ranked = (place == rank).astype(F32).astype(BF16)
            named = named + lax.dot_general(
                coded, ranked, (((1,), (1,)), ((), ())), preferred_element_type=F32
            )
            seen = seen + counts[:, 128:]
        return seen, named

    def copy_slots(g):
        return pltpu.make_async_copy(slots.at[g], slots_s.at[g], sems.at[3 + lax.rem(g, DELAY)])

    def place_team(g):
        for i in range(TEAM):
            for j in range(128):
                row = g * (TEAM * 128) + (i * 128 + j)
                dealt[pl.ds(slots_s[g, i, j], 1), :] = wide[pl.ds(row, 1), :]

    start = jnp.zeros((devices, 128), F32)
    carry = start, start
    for g in range(DELAY):
        carry = rank_team(g, carry)
        copy_slots(g).start()
    loads[2].wait()

    @pl.loop(0, rows // 64, unroll=4)
    def _(c):
        at = pl.ds(pl.multiple_of(c * 64, 64), 64)
        wide[at, :] = heights[at, :].astype(F32)

    def overlap(g, carry):
        copy_slots(g - DELAY).wait()
        place_team(g - DELAY)
        carry = rank_team(g, carry)
        copy_slots(g).start()
        return carry

    _, named = lax.fori_loop(DELAY, groups, overlap, carry)
    ids[...] = named

    @pl.loop(0, devices, unroll=8)
    def _(t):
        dealt[pl.ds(t * BLOCK + CAP, 1), :] = ids[pl.ds(t, 1), :]

    for g in range(groups - DELAY, groups):
        copy_slots(g).wait()
        place_team(g)

    part = devices // PARTS
    stores = []
    for i in range(PARTS):

        @pl.loop(i * part, (i + 1) * part, unroll=4)
        def _(t):
            packed[t] = dealt[pl.ds(pl.multiple_of(t * BLOCK, 8), BLOCK), :].astype(BF16)

        at = pl.ds(i * part, part)
        stores.append(pltpu.make_async_copy(packed.at[at], out.at[at], sems.at[3 + DELAY + i]))
        stores[-1].start()
    for store in stores:
        store.wait()


def bin_kernel(got, gap_mask, out, one, two, acc, codes, lines):
    devices = got.shape[0]
    tile_rows, tile_cols = gap_mask.shape
    quarters = tile_cols // 128
    pairs = devices // 2
    low = iota((1, 128), 1) < CAP
    for p in range(pairs):
        a = got[2 * p][CAP:CAP + 1, :].astype(F32)
        b = got[2 * p + 1][CAP:CAP + 1, :].astype(F32)
        codes[p:p + 1, :] = jnp.where(low, a, b)
    code = codes[...]
    shift = jnp.zeros(code.shape, I32)
    for j in range(1, 8):
        shift = shift + (code >= 128.0 * 2**j).astype(I32)
    seg = (shift << 7) + (code.astype(I32) >> shift) - 128
    for q in range(quarters):
        lines[q] = jnp.where((code > 0.0) & ((seg & (quarters - 1)) == q), seg // quarters, -1)
    line = iota((tile_rows, 128), 0)
    ones = jnp.ones((GROUP * CAP, 128), BF16)

    def group(i, fresh):
        cells = jnp.concatenate([got[GROUP * i + j][:CAP, :] for j in range(GROUP)], axis=0)
        cells = jnp.concatenate([cells, ones], axis=1)
        for q in range(quarters):
            hot = jnp.concatenate(
                [
                    (line == lines[q, pl.ds(GROUP // 2 * i + j, 1), :]).astype(F32).astype(BF16)
                    for j in range(GROUP // 2)
                ],
                axis=1,
            )
            part = jnp.dot(hot, cells, preferred_element_type=F32)
            acc[q] = part if fresh else acc[q] + part

    group(0, True)

    @pl.loop(1, devices // GROUP)
    def _(i):
        group(i, False)

    for q in range(quarters):
        cols = slice(q * 128, (q + 1) * 128)
        total = acc[q]
        summed, counted = total[:, :128], total[:, 128:]
        unknown = (gap_mask[:, cols] == 1) | (counted == 0.0)
        out[:, cols] = jnp.where(unknown, GAP, summed / jnp.maximum(counted, 1.0))
    odd = lax.axis_index("east") % 2 == 1
    first, last = out[:HALO, :], out[tile_rows - HALO:, :]
    one[...] = jnp.where(odd, last, first)
    two[...] = jnp.where(odd, first, last)


def lay_rows(slab, tile, above, below, cols):
    rows = tile.shape[0]
    tall = slab.shape[0]
    slab[:rows, :] = tile[:, cols]
    slab[rows:rows + HALO, :] = above[:, cols]
    slab[rows + HALO:tall - HALO, :] = jnp.zeros((tall - rows - 2 * HALO, 128), F32)
    slab[tall - HALO:, :] = below[:, cols]


def upper_lower(axis, one, two):
    odd = lax.axis_index(axis) % 2 == 1
    return jnp.where(odd, one, two), jnp.where(odd, two, one)


def sides_kernel(tile, got_one, got_two, one, two, slab):
    cols = tile.shape[1]
    lanes = slab.shape[0] // 128
    above, below = upper_lower("east", got_one[...], got_two[...])
    odd = lax.axis_index("north") % 2 == 1
    strips = []
    for at, keep in ((0, 0), (cols - 128, 128 - HALO)):
        lay_rows(slab, tile, above, below, slice(at, at + 128))
        strips.append(
            [
                slab[pl.ds(k, 128, stride=lanes), :].T[keep:keep + HALO, :]
                for k in range(lanes)
            ]
        )
    for k in range(lanes):
        west, east = strips[0][k], strips[1][k]
        one[k] = jnp.where(odd, east, west)
        two[k] = jnp.where(odd, west, east)


def turn_kernel(tile, east_one, east_two, coded, slabs, turned):
    cols = tile.shape[1]
    deep, lanes, _, _ = coded.shape
    above, below = upper_lower("east", east_one[...], east_two[...])
    for q in range(cols // 128):
        at = slice(q * 128, (q + 1) * 128)
        lay_rows(slabs.at[q], tile, above, below, at)
        for k in range(lanes):
            turned[k, at, :] = slabs[q, pl.ds(k, 128, stride=lanes), :].T
    for k in range(lanes):
        turned[k, cols:, :] = jnp.zeros((2 * HALO, 128), F32)
    for v in range(deep):
        for k in range(lanes):
            coded[v, k] = turned[k, pl.ds(v, 8, stride=deep), :]


def fill_kernel(coded, north_one, north_two, filled, totals, halo, cells, rate):
    deep, lanes, _, _ = coded.shape
    long = 8 * deep
    cols = long - 2 * HALO
    right, left = upper_lower("north", north_one[...], north_two[...])
    for k in range(lanes):
        halo[k, cols:cols + HALO, :] = right[k]
        halo[k, cols + HALO:, :] = left[k]
    for v in range(deep):
        column = iota((8, 128), 0) * deep + v
        for k in range(lanes):
            values = coded[v, k]
            if 7 * deep + v >= cols:
                beyond = halo[k, pl.ds(v, 8, stride=deep), :]
                values = jnp.where(column >= cols, beyond, values)
            unknown = values > 0.5 * GAP
            cells[v, k] = jnp.where(unknown, 0.0, values)
            rate[v, k] = jnp.where(unknown, 0.9 * 0.25, 0.0)

    def step(_, carry):
        opening = [cells[0, k] for k in range(lanes)]
        before = [pltpu.roll(cells[deep - 1, k], 1, axis=0) for k in range(lanes)]
        here = opening
        for v in range(deep):
            if v + 1 < deep:
                after = [cells[v + 1, k] for k in range(lanes)]
            else:
                after = [pltpu.roll(values, 7, axis=0) for values in opening]
            lower = [pltpu.roll(here[-1], 1, axis=1)] + here[:-1]
            upper = here[1:] + [pltpu.roll(here[0], 127, axis=1)]
            for k in range(lanes):
                total = (before[k] + after[k]) + (lower[k] + upper[k])
                cells[v, k] = here[k] + rate[v, k] * (total - 4.0 * here[k])
            before, here = here, after
        return carry

    lax.fori_loop(0, STEPS, step, 0, unroll=2)

    sums = [jnp.zeros((8, 128), F32) for _ in range(lanes)]
    for v in range(deep):
        inside = iota((8, 128), 0) * deep + v < cols
        for k in range(lanes):
            filled[v, k] = cells[v, k]
            soft = softplus(cells[v, k])
            sums[k] = sums[k] + (soft if 7 * deep + v < cols else jnp.where(inside, soft, 0.0))
    packed = jnp.zeros((8, 128), F32)
    for k in range(lanes):
        total = jnp.sum(sums[k], axis=0, keepdims=True)
        packed = packed + jnp.where(iota((8, 128), 0) == k, total, 0.0)
    for n in range(totals.shape[0]):
        totals[n] = packed


def depth_kernel(cells, surface_out, depths, surface, slabs, turned, sem):
    rows, cols = surface.shape
    quarters = cols // 128
    lanes = turned.shape[0]
    deep = cells.shape[0]
    for v in range(deep):
        for k in range(lanes):
            turned[k, pl.ds(v, 8, stride=deep), :] = cells[v, k]
    for q in range(quarters):
        at = slice(q * 128, (q + 1) * 128)
        for k in range(lanes):
            slabs[q, pl.ds(k, 128, stride=lanes), :] = turned[k, at, :].T
        surface[:, at] = slabs[q, :rows, :]
    store = pltpu.make_async_copy(surface, surface_out, sem)
    store.start()
    soft = softplus(surface[...])
    ahead = (iota((cols, cols), 0) < iota((cols, cols), 1)).astype(F32).astype(BF16)
    south = jnp.zeros((rows, cols), F32)
    for term in reversed(split(soft)):
        south = south + jnp.dot(term, ahead, preferred_element_type=F32)
    whole = south[:, cols - 1:] + soft[:, cols - 1:]
    depths[0] = south
    depths[1] = (whole - south) - soft
    store.wait()


def light_kernel(extinction, side, depths, totals, out, light, carried, sems):
    count, rows, cols = light.shape
    n_north = totals.shape[0]
    lanes = carried.shape[1] // 128
    here = lax.axis_index("north")
    zero = jnp.zeros((8, 128), F32)
    for k in range(2):
        total = zero
        for n in range(n_north):
            counts = here < n if k else here > n
            total = total + jnp.where(counts, totals[n], zero)
        turned = jnp.concatenate([total, jnp.zeros((120, 128), F32)], axis=0).T
        for lane in range(lanes):
            carried[k, pl.ds(lane, 128, stride=lanes), :] = jnp.broadcast_to(
                turned[:, lane:lane + 1], (128, 128)
            )

    def store(s, i):
        at = pl.ds(i * (rows // PIECES), rows // PIECES)
        return pltpu.make_async_copy(light.at[s, at], out.at[s, at], sems.at[s, i])

    @pl.loop(0, count)
    def _(s):
        pick = side[s]
        rate = extinction[s] * (-1.4426950408889634 / (cols * n_north))
        for i in range(PIECES):
            tall = slice(i * (rows // PIECES), (i + 1) * (rows // PIECES))
            for q in range(cols // 128):
                at = slice(q * 128, (q + 1) * 128)
                light[s, tall, at] = jnp.exp2(
                    rate * (depths[pick, tall, at] + carried[pick, tall, :])
                )
            store(s, i).start()

    @pl.loop(0, count)
    def _(s):
        for i in range(PIECES):
            store(s, i).wait()


def swapped(values, axis, start):
    count = lax.axis_size(axis)
    edges = [(i, i + 1) for i in range(start, count - 1, 2)]
    return lax.ppermute(values, axis, edges + [(j, i) for i, j in edges])


def body(heights, segment_ids, tile_owner, gap_mask, extinction, sun_side):
    rows_here = heights.shape[0]
    tile_rows, tile_cols = gap_mask.shape
    n_north = lax.axis_size("north")
    devices = lax.axis_size("east") * n_north
    chunks = rows_here // 128
    lanes = -(-(tile_rows + 2 * HALO) // 128)
    long = tile_cols + 2 * HALO
    mib = 1 << 20

    dealt = pl.pallas_call(
        deal_kernel,
        out_shape=jax.ShapeDtypeStruct((devices, BLOCK, 128), BF16),
        in_specs=[hbm()] * 3,
        out_specs=hbm(),
        scratch_shapes=[
            pltpu.VMEM((rows_here, 128), BF16),
            pltpu.VMEM((chunks, 128), I32),
            pltpu.VMEM((chunks, 128), I32),
            pltpu.VMEM((rows_here, 128), F32),
            pltpu.VMEM((devices * BLOCK, 128), F32),
            pltpu.VMEM((devices, BLOCK, 128), BF16),
            pltpu.VMEM((chunks // TEAM, 8, 128), I32),
            pltpu.VMEM((devices, 128), F32),
            pltpu.SMEM((chunks // TEAM, 8, 128), I32),
            pltpu.SemaphoreType.DMA((3 + DELAY + PARTS,)),
        ],
        compiler_params=pltpu.CompilerParams(vmem_limit_bytes=60 * mib),
        name="deal",
    )(heights, tile_owner.reshape(chunks, 128), segment_ids.reshape(chunks, 128))

    got = lax.all_to_all(dealt, ("east", "north"), split_axis=0, concat_axis=0, tiled=True)

    strip = jax.ShapeDtypeStruct((HALO, tile_cols), F32)
    tile, one, two = pl.pallas_call(
        bin_kernel,
        out_shape=(jax.ShapeDtypeStruct((tile_rows, tile_cols), F32), strip, strip),
        in_specs=[vmem()] * 2,
        out_specs=(vmem(),) * 3,
        scratch_shapes=[
            pltpu.VMEM((tile_cols // 128, tile_rows, 256), F32),
            pltpu.VMEM((devices // 2, 128), F32),
            pltpu.VMEM((tile_cols // 128, devices // 2, 128), I32),
        ],
        compiler_params=pltpu.CompilerParams(vmem_limit_bytes=24 * mib),
        name="bin",
    )(got, gap_mask)

    east = swapped(one, "east", 1), swapped(two, "east", 0)

    turned = jax.ShapeDtypeStruct((lanes, HALO, 128), F32)
    one, two = pl.pallas_call(
        sides_kernel,
        out_shape=(turned, turned),
        in_specs=[vmem()] * 3,
        out_specs=(vmem(),) * 2,
        scratch_shapes=[pltpu.VMEM((lanes * 128, 128), F32)],
        compiler_params=pltpu.CompilerParams(vmem_limit_bytes=16 * mib),
        name="sides",
    )(tile, *east)

    north = swapped(one, "north", 1), swapped(two, "north", 0)

    shape = jax.ShapeDtypeStruct((long // 8, lanes, 8, 128), F32)
    coded = pl.pallas_call(
        turn_kernel,
        out_shape=shape,
        in_specs=[vmem()] * 3,
        out_specs=vmem(),
        scratch_shapes=[
            pltpu.VMEM((tile_cols // 128, lanes * 128, 128), F32),
            pltpu.VMEM((lanes, long, 128), F32),
        ],
        compiler_params=pltpu.CompilerParams(vmem_limit_bytes=16 * mib),
        cost_estimate=pl.CostEstimate(
            flops=4 * tile_rows * tile_cols,
            bytes_accessed=16 * tile_rows * tile_cols,
            transcendentals=0,
        ),
        name="turn",
    )(tile, *east)

    cells, totals = pl.pallas_call(
        fill_kernel,
        out_shape=(shape, jax.ShapeDtypeStruct((n_north, 8, 128), F32)),
        in_specs=[vmem()] * 3,
        out_specs=(vmem(), vmem()),
        scratch_shapes=[pltpu.VMEM((lanes, long, 128), F32)] + [pltpu.VMEM(shape.shape, F32)] * 2,
        compiler_params=pltpu.CompilerParams(vmem_limit_bytes=32 * mib),
        name="fill",
    )(coded, *north)

    totals = lax.all_to_all(totals, "north", split_axis=0, concat_axis=0, tiled=True)

    surface, depths = pl.pallas_call(
        depth_kernel,
        out_shape=(
            jax.ShapeDtypeStruct((tile_rows, tile_cols), F32),
            jax.ShapeDtypeStruct((2, tile_rows, tile_cols), F32),
        ),
        in_specs=[vmem()],
        out_specs=(hbm(), vmem()),
        scratch_shapes=[
            pltpu.VMEM((tile_rows, tile_cols), F32),
            pltpu.VMEM((tile_cols // 128, lanes * 128, 128), F32),
            pltpu.VMEM((lanes, long, 128), F32),
            pltpu.SemaphoreType.DMA,
        ],
        compiler_params=pltpu.CompilerParams(vmem_limit_bytes=16 * mib),
        cost_estimate=pl.CostEstimate(
            flops=6 * tile_rows * tile_cols * tile_cols,
            bytes_accessed=16 * tile_rows * tile_cols,
            transcendentals=2 * tile_rows * tile_cols,
        ),
        name="depth",
    )(cells)

    light = pl.pallas_call(
        light_kernel,
        out_shape=jax.ShapeDtypeStruct((NS, tile_rows, tile_cols), F32),
        in_specs=[smem()] * 2 + [vmem()] * 2,
        out_specs=hbm(),
        scratch_shapes=[
            pltpu.VMEM((NS, tile_rows, tile_cols), F32),
            pltpu.VMEM((2, lanes * 128, 128), F32),
            pltpu.SemaphoreType.DMA((NS, PIECES)),
        ],
        compiler_params=pltpu.CompilerParams(vmem_limit_bytes=24 * mib),
        name="light",
    )(extinction, sun_side, depths, totals)
    return surface, light


def solution(mesh):
    return jax.shard_map(
        body,
        mesh=mesh,
        in_specs=(
            P(("east", "north"), None),
            P(("east", "north")),
            P(("east", "north"), None),
            P("east", "north"),
            P(),
            P(),
        ),
        out_specs=(P("east", "north"), P(None, "east", "north")),
        check_vma=False,
    )
```

```python
import jax
import jax.numpy as jnp
from jax import lax
from jax.experimental import pallas as pl
from jax.experimental.pallas import tpu as pltpu
from jax.sharding import PartitionSpec as P

NS = 8
STEPS = 20
CAP = 64
BLOCK = 72
HALO = 24
GAP = 1000.0
GROUP = 64
TEAM = 8
DELAY = 2
PIECES = 1

F32 = jnp.float32
BF16 = jnp.bfloat16
I32 = jnp.int32


def vmem():
    return pl.BlockSpec(memory_space=pltpu.VMEM)


def hbm():
    return pl.BlockSpec(memory_space=pltpu.HBM)


def pinned(values):
    return pltpu.with_memory_space_constraint(values, pltpu.HBM)


def smem():
    return pl.BlockSpec(memory_space=pltpu.SMEM)


def iota(shape, dim):
    return lax.broadcasted_iota(I32, shape, dim)


def split(values):
    terms = []
    for _ in range(3):
        term = values.astype(BF16)
        terms.append(term)
        values = values - term.astype(F32)
    return terms


def softplus(values):
    return jnp.log(1.0 + jnp.exp(values))


def deal_kernel(
    heights_in,
    owner_in,
    segment_in,
    out,
    heights,
    owner,
    segment,
    wide,
    dealt,
    slots,
    ids,
    slots_s,
    sems,
):
    devices = out.shape[0]
    rows = heights.shape[0]
    chunks = rows // 128
    groups = chunks // TEAM
    loads = [
        pltpu.make_async_copy(src, dst, sems.at[i])
        for i, (src, dst) in enumerate(
            ((owner_in, owner), (segment_in, segment), (heights_in, heights))
        )
    ]
    for load in loads:
        load.start()
    zeros = jnp.zeros((BLOCK, 128), F32)

    @pl.loop(0, devices, unroll=4)
    def _(t):
        dealt[pl.ds(pl.multiple_of(t * BLOCK, 8), BLOCK), :] = zeros

    tile = iota((devices, 128), 0)
    before = (iota((128, 256), 0) < iota((128, 256), 1)).astype(F32).astype(BF16)
    place = iota((128, 128), 0) & (CAP - 1)
    loads[0].wait()
    loads[1].wait()

    def rank_team(g, carry):
        seen, named = carry
        for i in range(TEAM):
            c = g * TEAM + i
            own = owner[pl.ds(c, 1), :]
            hit = tile == own
            counts = jnp.dot(hit.astype(F32).astype(BF16), before, preferred_element_type=F32)
            rank = jnp.sum(jnp.where(hit, counts[:, :128] + seen, 0.0), axis=0, keepdims=True)
            rank = rank.astype(I32)
            slots[g, i:i + 1, :] = own * BLOCK + rank
            seg = segment[pl.ds(c, 1), :]
            code = (((seg & 127) + 128) << (seg >> 7)).astype(F32)
            coded = jnp.where(hit, jnp.broadcast_to(code, hit.shape), 0.0).astype(BF16)
            ranked = (place == rank).astype(F32).astype(BF16)
            named = named + lax.dot_general(
                coded, ranked, (((1,), (1,)), ((), ())), preferred_element_type=F32
            )
            seen = seen + counts[:, 128:]
        return seen, named

    def copy_slots(g):
        return pltpu.make_async_copy(slots.at[g], slots_s.at[g], sems.at[3 + lax.rem(g, DELAY)])

    def place_team(g):
        for i in range(TEAM):
            for j in range(128):
                row = g * (TEAM * 128) + (i * 128 + j)
                dealt[pl.ds(slots_s[g, i, j], 1), :] = wide[pl.ds(row, 1), :]

    start = jnp.zeros((devices, 128), F32)
    carry = start, start
    for g in range(DELAY):
        carry = rank_team(g, carry)
        copy_slots(g).start()
    loads[2].wait()

    @pl.loop(0, rows // 64, unroll=4)
    def _(c):
        at = pl.ds(pl.multiple_of(c * 64, 64), 64)
        wide[at, :] = heights[at, :].astype(F32)

    def overlap(g, carry):
        copy_slots(g - DELAY).wait()
        place_team(g - DELAY)
        carry = rank_team(g, carry)
        copy_slots(g).start()
        return carry

    _, named = lax.fori_loop(DELAY, groups, overlap, carry)
    ids[...] = named

    @pl.loop(0, devices, unroll=8)
    def _(t):
        dealt[pl.ds(t * BLOCK + CAP, 1), :] = ids[pl.ds(t, 1), :]

    for g in range(groups - DELAY, groups):
        copy_slots(g).wait()
        place_team(g)

    @pl.loop(0, devices, unroll=4)
    def _(t):
        out[t] = dealt[pl.ds(pl.multiple_of(t * BLOCK, 8), BLOCK), :].astype(BF16)


def bin_kernel(got, gap_mask, out, one, two, acc, codes, lines):
    devices = got.shape[0]
    tile_rows, tile_cols = gap_mask.shape
    quarters = tile_cols // 128
    pairs = devices // 2
    low = iota((1, 128), 1) < CAP
    for p in range(pairs):
        a = got[2 * p][CAP:CAP + 1, :].astype(F32)
        b = got[2 * p + 1][CAP:CAP + 1, :].astype(F32)
        codes[p:p + 1, :] = jnp.where(low, a, b)
    code = codes[...]
    shift = jnp.zeros(code.shape, I32)
    for j in range(1, 8):
        shift = shift + (code >= 128.0 * 2**j).astype(I32)
    seg = (shift << 7) + (code.astype(I32) >> shift) - 128
    for q in range(quarters):
        lines[q] = jnp.where((code > 0.0) & ((seg & (quarters - 1)) == q), seg // quarters, -1)
    line = iota((tile_rows, 128), 0)
    ones = jnp.ones((GROUP * CAP, 128), BF16)

    def group(i, fresh):
        cells = jnp.concatenate([got[GROUP * i + j][:CAP, :] for j in range(GROUP)], axis=0)
        cells = jnp.concatenate([cells, ones], axis=1)
        for q in range(quarters):
            hot = jnp.concatenate(
                [
                    (line == lines[q, pl.ds(GROUP // 2 * i + j, 1), :]).astype(F32).astype(BF16)
                    for j in range(GROUP // 2)
                ],
                axis=1,
            )
            part = jnp.dot(hot, cells, preferred_element_type=F32)
            acc[q] = part if fresh else acc[q] + part

    group(0, True)

    @pl.loop(1, devices // GROUP)
    def _(i):
        group(i, False)

    for q in range(quarters):
        cols = slice(q * 128, (q + 1) * 128)
        total = acc[q]
        summed, counted = total[:, :128], total[:, 128:]
        unknown = (gap_mask[:, cols] == 1) | (counted == 0.0)
        out[:, cols] = jnp.where(unknown, GAP, summed / jnp.maximum(counted, 1.0))
    odd = lax.axis_index("east") % 2 == 1
    first, last = out[:HALO, :], out[tile_rows - HALO:, :]
    one[...] = jnp.where(odd, last, first)
    two[...] = jnp.where(odd, first, last)


def lay_rows(slab, tile, above, below, cols):
    rows = tile.shape[0]
    tall = slab.shape[0]
    slab[:rows, :] = tile[:, cols]
    slab[rows:rows + HALO, :] = above[:, cols]
    slab[rows + HALO:tall - HALO, :] = jnp.zeros((tall - rows - 2 * HALO, 128), F32)
    slab[tall - HALO:, :] = below[:, cols]


def upper_lower(axis, one, two):
    odd = lax.axis_index(axis) % 2 == 1
    return jnp.where(odd, one, two), jnp.where(odd, two, one)


def sides_kernel(tile, got_one, got_two, one, two, slab):
    cols = tile.shape[1]
    lanes = slab.shape[0] // 128
    above, below = upper_lower("east", got_one[...], got_two[...])
    odd = lax.axis_index("north") % 2 == 1
    strips = []
    for at, keep in ((0, 0), (cols - 128, 128 - HALO)):
        lay_rows(slab, tile, above, below, slice(at, at + 128))
        strips.append(
            [
                slab[pl.ds(k, 128, stride=lanes), :].T[keep:keep + HALO, :]
                for k in range(lanes)
            ]
        )
    for k in range(lanes):
        west, east = strips[0][k], strips[1][k]
        one[k] = jnp.where(odd, east, west)
        two[k] = jnp.where(odd, west, east)


def turn_kernel(tile, east_one, east_two, coded, slabs, turned):
    cols = tile.shape[1]
    deep, lanes, _, _ = coded.shape
    above, below = upper_lower("east", east_one[...], east_two[...])
    for q in range(cols // 128):
        at = slice(q * 128, (q + 1) * 128)
        lay_rows(slabs.at[q], tile, above, below, at)
        for k in range(lanes):
            turned[k, at, :] = slabs[q, pl.ds(k, 128, stride=lanes), :].T
    for k in range(lanes):
        turned[k, cols:, :] = jnp.zeros((2 * HALO, 128), F32)
    for v in range(deep):
        for k in range(lanes):
            coded[v, k] = turned[k, pl.ds(v, 8, stride=deep), :]


def fill_kernel(coded, north_one, north_two, filled, totals, halo, cells, rate):
    deep, lanes, _, _ = coded.shape
    long = 8 * deep
    cols = long - 2 * HALO
    right, left = upper_lower("north", north_one[...], north_two[...])
    for k in range(lanes):
        halo[k, cols:cols + HALO, :] = right[k]
        halo[k, cols + HALO:, :] = left[k]
    for v in range(deep):
        column = iota((8, 128), 0) * deep + v
        for k in range(lanes):
            values = coded[v, k]
            if 7 * deep + v >= cols:
                beyond = halo[k, pl.ds(v, 8, stride=deep), :]
                values = jnp.where(column >= cols, beyond, values)
            unknown = values > 0.5 * GAP
            cells[v, k] = jnp.where(unknown, 0.0, values)
            rate[v, k] = jnp.where(unknown, 0.9 * 0.25, 0.0)

    def step(_, carry):
        opening = [cells[0, k] for k in range(lanes)]
        before = [pltpu.roll(cells[deep - 1, k], 1, axis=0) for k in range(lanes)]
        here = opening
        for v in range(deep):
            if v + 1 < deep:
                after = [cells[v + 1, k] for k in range(lanes)]
            else:
                after = [pltpu.roll(values, 7, axis=0) for values in opening]
            lower = [pltpu.roll(here[-1], 1, axis=1)] + here[:-1]
            upper = here[1:] + [pltpu.roll(here[0], 127, axis=1)]
            for k in range(lanes):
                total = (before[k] + after[k]) + (lower[k] + upper[k])
                cells[v, k] = here[k] + rate[v, k] * (total - 4.0 * here[k])
            before, here = here, after
        return carry

    lax.fori_loop(0, STEPS, step, 0, unroll=2)

    sums = [jnp.zeros((8, 128), F32) for _ in range(lanes)]
    for v in range(deep):
        inside = iota((8, 128), 0) * deep + v < cols
        for k in range(lanes):
            filled[v, k] = cells[v, k]
            soft = softplus(cells[v, k])
            sums[k] = sums[k] + (soft if 7 * deep + v < cols else jnp.where(inside, soft, 0.0))
    packed = jnp.zeros((8, 128), F32)
    for k in range(lanes):
        total = jnp.sum(sums[k], axis=0, keepdims=True)
        packed = packed + jnp.where(iota((8, 128), 0) == k, total, 0.0)
    for n in range(totals.shape[0]):
        totals[n] = packed


def depth_kernel(cells, surface_out, depths, surface, slabs, turned, sem):
    rows, cols = surface.shape
    quarters = cols // 128
    lanes = turned.shape[0]
    deep = cells.shape[0]
    for v in range(deep):
        for k in range(lanes):
            turned[k, pl.ds(v, 8, stride=deep), :] = cells[v, k]
    for q in range(quarters):
        at = slice(q * 128, (q + 1) * 128)
        for k in range(lanes):
            slabs[q, pl.ds(k, 128, stride=lanes), :] = turned[k, at, :].T
        surface[:, at] = slabs[q, :rows, :]
    store = pltpu.make_async_copy(surface, surface_out, sem)
    store.start()
    soft = softplus(surface[...])
    ahead = (iota((cols, cols), 0) < iota((cols, cols), 1)).astype(F32).astype(BF16)
    south = jnp.zeros((rows, cols), F32)
    for term in reversed(split(soft)):
        south = south + jnp.dot(term, ahead, preferred_element_type=F32)
    whole = south[:, cols - 1:] + soft[:, cols - 1:]
    depths[0] = south
    depths[1] = (whole - south) - soft
    store.wait()


def light_kernel(extinction, side, depths, totals, out, light, carried, sems):
    count, rows, cols = light.shape
    n_north = totals.shape[0]
    lanes = carried.shape[1] // 128
    here = lax.axis_index("north")
    zero = jnp.zeros((8, 128), F32)
    for k in range(2):
        total = zero
        for n in range(n_north):
            counts = here < n if k else here > n
            total = total + jnp.where(counts, totals[n], zero)
        turned = jnp.concatenate([total, jnp.zeros((120, 128), F32)], axis=0).T
        for lane in range(lanes):
            carried[k, pl.ds(lane, 128, stride=lanes), :] = jnp.broadcast_to(
                turned[:, lane:lane + 1], (128, 128)
            )

    def store(s, i):
        at = pl.ds(i * (rows // PIECES), rows // PIECES)
        return pltpu.make_async_copy(light.at[s, at], out.at[s, at], sems.at[s, i])

    @pl.loop(0, count)
    def _(s):
        pick = side[s]
        rate = extinction[s] * (-1.4426950408889634 / (cols * n_north))
        for i in range(PIECES):
            tall = slice(i * (rows // PIECES), (i + 1) * (rows // PIECES))
            for q in range(cols // 128):
                at = slice(q * 128, (q + 1) * 128)
                light[s, tall, at] = jnp.exp2(
                    rate * (depths[pick, tall, at] + carried[pick, tall, :])
                )
            store(s, i).start()

    @pl.loop(0, count)
    def _(s):
        for i in range(PIECES):
            store(s, i).wait()


def swapped(values, axis, start):
    count = lax.axis_size(axis)
    edges = [(i, i + 1) for i in range(start, count - 1, 2)]
    return lax.ppermute(values, axis, edges + [(j, i) for i, j in edges])


def body(heights, segment_ids, tile_owner, gap_mask, extinction, sun_side):
    rows_here = heights.shape[0]
    tile_rows, tile_cols = gap_mask.shape
    n_north = lax.axis_size("north")
    devices = lax.axis_size("east") * n_north
    chunks = rows_here // 128
    lanes = -(-(tile_rows + 2 * HALO) // 128)
    long = tile_cols + 2 * HALO
    mib = 1 << 20

    dealt = pl.pallas_call(
        deal_kernel,
        out_shape=jax.ShapeDtypeStruct((devices, BLOCK, 128), BF16),
        in_specs=[hbm()] * 3,
        out_specs=vmem(),
        scratch_shapes=[
            pltpu.VMEM((rows_here, 128), BF16),
            pltpu.VMEM((chunks, 128), I32),
            pltpu.VMEM((chunks, 128), I32),
            pltpu.VMEM((rows_here, 128), F32),
            pltpu.VMEM((devices * BLOCK, 128), F32),
            pltpu.VMEM((chunks // TEAM, 8, 128), I32),
            pltpu.VMEM((devices, 128), F32),
            pltpu.SMEM((chunks // TEAM, 8, 128), I32),
            pltpu.SemaphoreType.DMA((3 + DELAY,)),
        ],
        compiler_params=pltpu.CompilerParams(vmem_limit_bytes=24 * mib),
        name="deal",
    )(*map(pinned, (heights, tile_owner.reshape(chunks, 128), segment_ids.reshape(chunks, 128))))

    got = lax.all_to_all(dealt, ("east", "north"), split_axis=0, concat_axis=0, tiled=True)

    strip = jax.ShapeDtypeStruct((HALO, tile_cols), F32)
    tile, one, two = pl.pallas_call(
        bin_kernel,
        out_shape=(jax.ShapeDtypeStruct((tile_rows, tile_cols), F32), strip, strip),
        in_specs=[vmem()] * 2,
        out_specs=(vmem(),) * 3,
        scratch_shapes=[
            pltpu.VMEM((tile_cols // 128, tile_rows, 256), F32),
            pltpu.VMEM((devices // 2, 128), F32),
            pltpu.VMEM((tile_cols // 128, devices // 2, 128), I32),
        ],
        compiler_params=pltpu.CompilerParams(vmem_limit_bytes=24 * mib),
        name="bin",
    )(got, gap_mask)

    east = swapped(one, "east", 1), swapped(two, "east", 0)

    turned = jax.ShapeDtypeStruct((lanes, HALO, 128), F32)
    one, two = pl.pallas_call(
        sides_kernel,
        out_shape=(turned, turned),
        in_specs=[vmem()] * 3,
        out_specs=(vmem(),) * 2,
        scratch_shapes=[pltpu.VMEM((lanes * 128, 128), F32)],
        compiler_params=pltpu.CompilerParams(vmem_limit_bytes=16 * mib),
        name="sides",
    )(tile, *east)

    north = swapped(one, "north", 1), swapped(two, "north", 0)

    shape = jax.ShapeDtypeStruct((long // 8, lanes, 8, 128), F32)
    coded = pl.pallas_call(
        turn_kernel,
        out_shape=shape,
        in_specs=[vmem()] * 3,
        out_specs=vmem(),
        scratch_shapes=[
            pltpu.VMEM((tile_cols // 128, lanes * 128, 128), F32),
            pltpu.VMEM((lanes, long, 128), F32),
        ],
        compiler_params=pltpu.CompilerParams(vmem_limit_bytes=16 * mib),
        cost_estimate=pl.CostEstimate(
            flops=4 * tile_rows * tile_cols,
            bytes_accessed=16 * tile_rows * tile_cols,
            transcendentals=0,
        ),
        name="turn",
    )(tile, *east)

    cells, totals = pl.pallas_call(
        fill_kernel,
        out_shape=(shape, jax.ShapeDtypeStruct((n_north, 8, 128), F32)),
        in_specs=[vmem()] * 3,
        out_specs=(vmem(), vmem()),
        scratch_shapes=[pltpu.VMEM((lanes, long, 128), F32)] + [pltpu.VMEM(shape.shape, F32)] * 2,
        compiler_params=pltpu.CompilerParams(vmem_limit_bytes=32 * mib),
        name="fill",
    )(coded, *north)

    totals = lax.all_to_all(totals, "north", split_axis=0, concat_axis=0, tiled=True)

    surface, depths = pl.pallas_call(
        depth_kernel,
        out_shape=(
            jax.ShapeDtypeStruct((tile_rows, tile_cols), F32),
            jax.ShapeDtypeStruct((2, tile_rows, tile_cols), F32),
        ),
        in_specs=[vmem()],
        out_specs=(hbm(), vmem()),
        scratch_shapes=[
            pltpu.VMEM((tile_rows, tile_cols), F32),
            pltpu.VMEM((tile_cols // 128, lanes * 128, 128), F32),
            pltpu.VMEM((lanes, long, 128), F32),
            pltpu.SemaphoreType.DMA,
        ],
        compiler_params=pltpu.CompilerParams(vmem_limit_bytes=16 * mib),
        cost_estimate=pl.CostEstimate(
            flops=6 * tile_rows * tile_cols * tile_cols,
            bytes_accessed=16 * tile_rows * tile_cols,
            transcendentals=2 * tile_rows * tile_cols,
        ),
        name="depth",
    )(cells)

    light = pl.pallas_call(
        light_kernel,
        out_shape=jax.ShapeDtypeStruct((NS, tile_rows, tile_cols), F32),
        in_specs=[smem()] * 2 + [vmem()] * 2,
        out_specs=hbm(),
        scratch_shapes=[
            pltpu.VMEM((NS, tile_rows, tile_cols), F32),
            pltpu.VMEM((2, lanes * 128, 128), F32),
            pltpu.SemaphoreType.DMA((NS, PIECES)),
        ],
        compiler_params=pltpu.CompilerParams(vmem_limit_bytes=24 * mib),
        name="light",
    )(extinction, sun_side, depths, totals)
    return surface, light


def solution(mesh):
    return jax.shard_map(
        body,
        mesh=mesh,
        in_specs=(
            P(("east", "north"), None),
            P(("east", "north")),
            P(("east", "north"), None),
            P("east", "north"),
            P(),
            P(),
        ),
        out_specs=(P("east", "north"), P(None, "east", "north")),
        check_vma=False,
    )
```

```python
import jax
import jax.numpy as jnp
from jax import lax
from jax.experimental import pallas as pl
from jax.experimental.pallas import tpu as pltpu
from jax.sharding import PartitionSpec as P

NS = 8
STEPS = 20
CAP = 64
BLOCK = 72
HALO = 24
GAP = 1000.0
GROUP = 64
TEAM = 8
DELAY = 2
PIECES = 1

F32 = jnp.float32
BF16 = jnp.bfloat16
I32 = jnp.int32


def vmem():
    return pl.BlockSpec(memory_space=pltpu.VMEM)


def hbm():
    return pl.BlockSpec(memory_space=pltpu.HBM)


def pinned(values):
    return pltpu.with_memory_space_constraint(values, pltpu.HBM)


def smem():
    return pl.BlockSpec(memory_space=pltpu.SMEM)


def iota(shape, dim):
    return lax.broadcasted_iota(I32, shape, dim)


def split(values):
    terms = []
    for _ in range(3):
        term = values.astype(BF16)
        terms.append(term)
        values = values - term.astype(F32)
    return terms


def softplus(values):
    return jnp.log(1.0 + jnp.exp(values))


def deal_kernel(
    heights_in,
    owner_in,
    segment_in,
    out,
    heights,
    owner,
    segment,
    wide,
    dealt,
    slots,
    ids,
    slots_s,
    sems,
):
    devices = out.shape[0]
    rows = heights.shape[0]
    chunks = rows // 128
    groups = chunks // TEAM
    loads = [
        pltpu.make_async_copy(src, dst, sems.at[i])
        for i, (src, dst) in enumerate(
            ((owner_in, owner), (segment_in, segment), (heights_in, heights))
        )
    ]
    for load in loads:
        load.start()
    zeros = jnp.zeros((BLOCK, 128), F32)

    @pl.loop(0, devices, unroll=8)
    def _(t):
        dealt[pl.ds(pl.multiple_of(t * BLOCK, 8), BLOCK), :] = zeros

    tile = iota((devices, 128), 0)
    before = (iota((128, 256), 0) < iota((128, 256), 1)).astype(F32).astype(BF16)
    place = iota((128, 128), 0) & (CAP - 1)
    loads[0].wait()
    loads[1].wait()

    def rank_team(g, carry):
        seen, named = carry
        for i in range(TEAM):
            c = g * TEAM + i
            own = owner[pl.ds(c, 1), :]
            hit = tile == own
            counts = jnp.dot(hit.astype(F32).astype(BF16), before, preferred_element_type=F32)
            rank = jnp.sum(jnp.where(hit, counts[:, :128] + seen, 0.0), axis=0, keepdims=True)
            rank = rank.astype(I32)
            slots[g, i:i + 1, :] = own * BLOCK + rank
            seg = segment[pl.ds(c, 1), :]
            code = (((seg & 127) + 128) << (seg >> 7)).astype(F32)
            coded = jnp.where(hit, jnp.broadcast_to(code, hit.shape), 0.0).astype(BF16)
            ranked = (place == rank).astype(F32).astype(BF16)
            named = named + lax.dot_general(
                coded, ranked, (((1,), (1,)), ((), ())), preferred_element_type=F32
            )
            seen = seen + counts[:, 128:]
        return seen, named

    def copy_slots(g):
        return pltpu.make_async_copy(slots.at[g], slots_s.at[g], sems.at[3 + lax.rem(g, DELAY)])

    def place_team(g):
        for i in range(TEAM):
            for j in range(128):
                row = g * (TEAM * 128) + (i * 128 + j)
                dealt[pl.ds(slots_s[g, i, j], 1), :] = wide[pl.ds(row, 1), :]

    start = jnp.zeros((devices, 128), F32)
    carry = start, start
    for g in range(DELAY):
        carry = rank_team(g, carry)
        copy_slots(g).start()
    loads[2].wait()

    @pl.loop(0, rows // 64, unroll=8)
    def _(c):
        at = pl.ds(pl.multiple_of(c * 64, 64), 64)
        wide[at, :] = heights[at, :].astype(F32)

    def overlap(g, carry):
        copy_slots(g - DELAY).wait()
        place_team(g - DELAY)
        carry = rank_team(g, carry)
        copy_slots(g).start()
        return carry

    _, named = lax.fori_loop(DELAY, groups, overlap, carry)
    ids[...] = named

    @pl.loop(0, devices, unroll=8)
    def _(t):
        dealt[pl.ds(t * BLOCK + CAP, 1), :] = ids[pl.ds(t, 1), :]

    for g in range(groups - DELAY, groups):
        copy_slots(g).wait()
        place_team(g)

    @pl.loop(0, devices, unroll=8)
    def _(t):
        out[t] = dealt[pl.ds(pl.multiple_of(t * BLOCK, 8), BLOCK), :].astype(BF16)


def bin_kernel(got, gap_mask, out, one, two, acc, codes, lines):
    devices = got.shape[0]
    tile_rows, tile_cols = gap_mask.shape
    quarters = tile_cols // 128
    pairs = devices // 2
    low = iota((1, 128), 1) < CAP
    for p in range(pairs):
        a = got[2 * p][CAP:CAP + 1, :].astype(F32)
        b = got[2 * p + 1][CAP:CAP + 1, :].astype(F32)
        codes[p:p + 1, :] = jnp.where(low, a, b)
    code = codes[...]
    shift = jnp.zeros(code.shape, I32)
    for j in range(1, 8):
        shift = shift + (code >= 128.0 * 2**j).astype(I32)
    seg = (shift << 7) + (code.astype(I32) >> shift) - 128
    for q in range(quarters):
        lines[q] = jnp.where((code > 0.0) & ((seg & (quarters - 1)) == q), seg // quarters, -1)
    line = iota((tile_rows, 128), 0)
    ones = jnp.ones((GROUP * CAP, 128), BF16)

    def group(i, fresh):
        cells = jnp.concatenate([got[GROUP * i + j][:CAP, :] for j in range(GROUP)], axis=0)
        cells = jnp.concatenate([cells, ones], axis=1)
        for q in range(quarters):
            hot = jnp.concatenate(
                [
                    (line == lines[q, pl.ds(GROUP // 2 * i + j, 1), :]).astype(F32).astype(BF16)
                    for j in range(GROUP // 2)
                ],
                axis=1,
            )
            part = jnp.dot(hot, cells, preferred_element_type=F32)
            acc[q] = part if fresh else acc[q] + part

    group(0, True)

    @pl.loop(1, devices // GROUP)
    def _(i):
        group(i, False)

    for q in range(quarters):
        cols = slice(q * 128, (q + 1) * 128)
        total = acc[q]
        summed, counted = total[:, :128], total[:, 128:]
        unknown = (gap_mask[:, cols] == 1) | (counted == 0.0)
        out[:, cols] = jnp.where(unknown, GAP, summed / jnp.maximum(counted, 1.0))
    odd = lax.axis_index("east") % 2 == 1
    first, last = out[:HALO, :], out[tile_rows - HALO:, :]
    one[...] = jnp.where(odd, last, first)
    two[...] = jnp.where(odd, first, last)


def lay_rows(slab, tile, above, below, cols):
    rows = tile.shape[0]
    tall = slab.shape[0]
    slab[:rows, :] = tile[:, cols]
    slab[rows:rows + HALO, :] = above[:, cols]
    slab[rows + HALO:tall - HALO, :] = jnp.zeros((tall - rows - 2 * HALO, 128), F32)
    slab[tall - HALO:, :] = below[:, cols]


def upper_lower(axis, one, two):
    odd = lax.axis_index(axis) % 2 == 1
    return jnp.where(odd, one, two), jnp.where(odd, two, one)


def sides_kernel(tile, got_one, got_two, one, two, slab):
    cols = tile.shape[1]
    lanes = slab.shape[0] // 128
    above, below = upper_lower("east", got_one[...], got_two[...])
    odd = lax.axis_index("north") % 2 == 1
    strips = []
    for at, keep in ((0, 0), (cols - 128, 128 - HALO)):
        lay_rows(slab, tile, above, below, slice(at, at + 128))
        strips.append(
            [
                slab[pl.ds(k, 128, stride=lanes), :].T[keep:keep + HALO, :]
                for k in range(lanes)
            ]
        )
    for k in range(lanes):
        west, east = strips[0][k], strips[1][k]
        one[k] = jnp.where(odd, east, west)
        two[k] = jnp.where(odd, west, east)


def turn_kernel(tile, east_one, east_two, coded, slabs, turned):
    cols = tile.shape[1]
    deep, lanes, _, _ = coded.shape
    above, below = upper_lower("east", east_one[...], east_two[...])
    for q in range(cols // 128):
        at = slice(q * 128, (q + 1) * 128)
        lay_rows(slabs.at[q], tile, above, below, at)
        for k in range(lanes):
            turned[k, at, :] = slabs[q, pl.ds(k, 128, stride=lanes), :].T
    for k in range(lanes):
        turned[k, cols:, :] = jnp.zeros((2 * HALO, 128), F32)
    for v in range(deep):
        for k in range(lanes):
            coded[v, k] = turned[k, pl.ds(v, 8, stride=deep), :]


def fill_kernel(coded, north_one, north_two, filled, totals, halo, cells, rate):
    deep, lanes, _, _ = coded.shape
    long = 8 * deep
    cols = long - 2 * HALO
    right, left = upper_lower("north", north_one[...], north_two[...])
    for k in range(lanes):
        halo[k, cols:cols + HALO, :] = right[k]
        halo[k, cols + HALO:, :] = left[k]
    for v in range(deep):
        column = iota((8, 128), 0) * deep + v
        for k in range(lanes):
            values = coded[v, k]
            if 7 * deep + v >= cols:
                beyond = halo[k, pl.ds(v, 8, stride=deep), :]
                values = jnp.where(column >= cols, beyond, values)
            unknown = values > 0.5 * GAP
            cells[v, k] = jnp.where(unknown, 0.0, values)
            rate[v, k] = jnp.where(unknown, 0.9 * 0.25, 0.0)

    def step(_, carry):
        opening = [cells[0, k] for k in range(lanes)]
        before = [pltpu.roll(cells[deep - 1, k], 1, axis=0) for k in range(lanes)]
        here = opening
        for v in range(deep):
            if v + 1 < deep:
                after = [cells[v + 1, k] for k in range(lanes)]
            else:
                after = [pltpu.roll(values, 7, axis=0) for values in opening]
            lower = [pltpu.roll(here[-1], 1, axis=1)] + here[:-1]
            upper = here[1:] + [pltpu.roll(here[0], 127, axis=1)]
            for k in range(lanes):
                total = (before[k] + after[k]) + (lower[k] + upper[k])
                cells[v, k] = here[k] + rate[v, k] * (total - 4.0 * here[k])
            before, here = here, after
        return carry

    lax.fori_loop(0, STEPS, step, 0, unroll=4)

    sums = [jnp.zeros((8, 128), F32) for _ in range(lanes)]
    for v in range(deep):
        inside = iota((8, 128), 0) * deep + v < cols
        for k in range(lanes):
            filled[v, k] = cells[v, k]
            soft = softplus(cells[v, k])
            sums[k] = sums[k] + (soft if 7 * deep + v < cols else jnp.where(inside, soft, 0.0))
    packed = jnp.zeros((8, 128), F32)
    for k in range(lanes):
        total = jnp.sum(sums[k], axis=0, keepdims=True)
        packed = packed + jnp.where(iota((8, 128), 0) == k, total, 0.0)
    for n in range(totals.shape[0]):
        totals[n] = packed


def depth_kernel(cells, surface_out, depths, surface, slabs, turned, sem):
    rows, cols = surface.shape
    quarters = cols // 128
    lanes = turned.shape[0]
    deep = cells.shape[0]
    for v in range(deep):
        for k in range(lanes):
            turned[k, pl.ds(v, 8, stride=deep), :] = cells[v, k]
    for q in range(quarters):
        at = slice(q * 128, (q + 1) * 128)
        for k in range(lanes):
            slabs[q, pl.ds(k, 128, stride=lanes), :] = turned[k, at, :].T
        surface[:, at] = slabs[q, :rows, :]
    store = pltpu.make_async_copy(surface, surface_out, sem)
    store.start()
    soft = softplus(surface[...])
    ahead = (iota((cols, cols), 0) < iota((cols, cols), 1)).astype(F32).astype(BF16)
    south = jnp.zeros((rows, cols), F32)
    for term in reversed(split(soft)):
        south = south + jnp.dot(term, ahead, preferred_element_type=F32)
    whole = south[:, cols - 1:] + soft[:, cols - 1:]
    depths[0] = south
    depths[1] = (whole - south) - soft
    store.wait()


def light_kernel(extinction, side, depths, totals, out, light, carried, sems):
    count, rows, cols = light.shape
    n_north = totals.shape[0]
    lanes = carried.shape[1] // 128
    here = lax.axis_index("north")
    zero = jnp.zeros((8, 128), F32)
    for k in range(2):
        total = zero
        for n in range(n_north):
            counts = here < n if k else here > n
            total = total + jnp.where(counts, totals[n], zero)
        turned = jnp.concatenate([total, jnp.zeros((120, 128), F32)], axis=0).T
        for lane in range(lanes):
            carried[k, pl.ds(lane, 128, stride=lanes), :] = jnp.broadcast_to(
                turned[:, lane:lane + 1], (128, 128)
            )

    def store(s, i):
        at = pl.ds(i * (rows // PIECES), rows // PIECES)
        return pltpu.make_async_copy(light.at[s, at], out.at[s, at], sems.at[s, i])

    @pl.loop(0, count)
    def _(s):
        pick = side[s]
        rate = extinction[s] * (-1.4426950408889634 / (cols * n_north))
        for i in range(PIECES):
            tall = slice(i * (rows // PIECES), (i + 1) * (rows // PIECES))
            for q in range(cols // 128):
                at = slice(q * 128, (q + 1) * 128)
                light[s, tall, at] = jnp.exp2(
                    rate * (depths[pick, tall, at] + carried[pick, tall, :])
                )
            store(s, i).start()

    @pl.loop(0, count)
    def _(s):
        for i in range(PIECES):
            store(s, i).wait()


def swapped(values, axis, start):
    count = lax.axis_size(axis)
    edges = [(i, i + 1) for i in range(start, count - 1, 2)]
    return lax.ppermute(values, axis, edges + [(j, i) for i, j in edges])


def body(heights, segment_ids, tile_owner, gap_mask, extinction, sun_side):
    rows_here = heights.shape[0]
    tile_rows, tile_cols = gap_mask.shape
    n_north = lax.axis_size("north")
    devices = lax.axis_size("east") * n_north
    chunks = rows_here // 128
    lanes = -(-(tile_rows + 2 * HALO) // 128)
    long = tile_cols + 2 * HALO
    mib = 1 << 20

    dealt = pl.pallas_call(
        deal_kernel,
        out_shape=jax.ShapeDtypeStruct((devices, BLOCK, 128), BF16),
        in_specs=[hbm()] * 3,
        out_specs=vmem(),
        scratch_shapes=[
            pltpu.VMEM((rows_here, 128), BF16),
            pltpu.VMEM((chunks, 128), I32),
            pltpu.VMEM((chunks, 128), I32),
            pltpu.VMEM((rows_here, 128), F32),
            pltpu.VMEM((devices * BLOCK, 128), F32),
            pltpu.VMEM((chunks // TEAM, 8, 128), I32),
            pltpu.VMEM((devices, 128), F32),
            pltpu.SMEM((chunks // TEAM, 8, 128), I32),
            pltpu.SemaphoreType.DMA((3 + DELAY,)),
        ],
        compiler_params=pltpu.CompilerParams(vmem_limit_bytes=24 * mib),
        name="deal",
    )(*map(pinned, (heights, tile_owner.reshape(chunks, 128), segment_ids.reshape(chunks, 128))))

    got = lax.all_to_all(dealt, ("east", "north"), split_axis=0, concat_axis=0, tiled=True)

    strip = jax.ShapeDtypeStruct((HALO, tile_cols), F32)
    tile, one, two = pl.pallas_call(
        bin_kernel,
        out_shape=(jax.ShapeDtypeStruct((tile_rows, tile_cols), F32), strip, strip),
        in_specs=[vmem()] * 2,
        out_specs=(vmem(),) * 3,
        scratch_shapes=[
            pltpu.VMEM((tile_cols // 128, tile_rows, 256), F32),
            pltpu.VMEM((devices // 2, 128), F32),
            pltpu.VMEM((tile_cols // 128, devices // 2, 128), I32),
        ],
        compiler_params=pltpu.CompilerParams(vmem_limit_bytes=24 * mib),
        name="bin",
    )(got, gap_mask)

    east = swapped(one, "east", 1), swapped(two, "east", 0)

    turned = jax.ShapeDtypeStruct((lanes, HALO, 128), F32)
    one, two = pl.pallas_call(
        sides_kernel,
        out_shape=(turned, turned),
        in_specs=[vmem()] * 3,
        out_specs=(vmem(),) * 2,
        scratch_shapes=[pltpu.VMEM((lanes * 128, 128), F32)],
        compiler_params=pltpu.CompilerParams(vmem_limit_bytes=16 * mib),
        name="sides",
    )(tile, *east)

    north = swapped(one, "north", 1), swapped(two, "north", 0)

    shape = jax.ShapeDtypeStruct((long // 8, lanes, 8, 128), F32)
    coded = pl.pallas_call(
        turn_kernel,
        out_shape=shape,
        in_specs=[vmem()] * 3,
        out_specs=vmem(),
        scratch_shapes=[
            pltpu.VMEM((tile_cols // 128, lanes * 128, 128), F32),
            pltpu.VMEM((lanes, long, 128), F32),
        ],
        compiler_params=pltpu.CompilerParams(vmem_limit_bytes=16 * mib),
        cost_estimate=pl.CostEstimate(
            flops=4 * tile_rows * tile_cols,
            bytes_accessed=16 * tile_rows * tile_cols,
            transcendentals=0,
        ),
        name="turn",
    )(tile, *east)

    cells, totals = pl.pallas_call(
        fill_kernel,
        out_shape=(shape, jax.ShapeDtypeStruct((n_north, 8, 128), F32)),
        in_specs=[vmem()] * 3,
        out_specs=(vmem(), vmem()),
        scratch_shapes=[pltpu.VMEM((lanes, long, 128), F32)] + [pltpu.VMEM(shape.shape, F32)] * 2,
        compiler_params=pltpu.CompilerParams(vmem_limit_bytes=32 * mib),
        name="fill",
    )(coded, *north)

    totals = lax.all_to_all(totals, "north", split_axis=0, concat_axis=0, tiled=True)

    surface, depths = pl.pallas_call(
        depth_kernel,
        out_shape=(
            jax.ShapeDtypeStruct((tile_rows, tile_cols), F32),
            jax.ShapeDtypeStruct((2, tile_rows, tile_cols), F32),
        ),
        in_specs=[vmem()],
        out_specs=(hbm(), vmem()),
        scratch_shapes=[
            pltpu.VMEM((tile_rows, tile_cols), F32),
            pltpu.VMEM((tile_cols // 128, lanes * 128, 128), F32),
            pltpu.VMEM((lanes, long, 128), F32),
            pltpu.SemaphoreType.DMA,
        ],
        compiler_params=pltpu.CompilerParams(vmem_limit_bytes=16 * mib),
        cost_estimate=pl.CostEstimate(
            flops=6 * tile_rows * tile_cols * tile_cols,
            bytes_accessed=16 * tile_rows * tile_cols,
            transcendentals=2 * tile_rows * tile_cols,
        ),
        name="depth",
    )(cells)

    light = pl.pallas_call(
        light_kernel,
        out_shape=jax.ShapeDtypeStruct((NS, tile_rows, tile_cols), F32),
        in_specs=[smem()] * 2 + [vmem()] * 2,
        out_specs=hbm(),
        scratch_shapes=[
            pltpu.VMEM((NS, tile_rows, tile_cols), F32),
            pltpu.VMEM((2, lanes * 128, 128), F32),
            pltpu.SemaphoreType.DMA((NS, PIECES)),
        ],
        compiler_params=pltpu.CompilerParams(vmem_limit_bytes=24 * mib),
        name="light",
    )(extinction, sun_side, depths, totals)
    return surface, light


def solution(mesh):
    return jax.shard_map(
        body,
        mesh=mesh,
        in_specs=(
            P(("east", "north"), None),
            P(("east", "north")),
            P(("east", "north"), None),
            P("east", "north"),
            P(),
            P(),
        ),
        out_specs=(P("east", "north"), P(None, "east", "north")),
        check_vma=False,
    )
```
